128 devices in a mesh: section: 8 (over x, z_hi), dp: 16 (over y, z_lo, core).
Axes of the slice: x: 4, y: 4, z: 4 (z_hi: 2, z_lo: 2; z = z_hi * 2 + z_lo), core: 2. Of those that a mesh axis runs over, the one named last changes fastest.
Arguments:
- tokens: bfloat16 [2, 4, 896, 2048], P(None, None, 'dp'), may hold values from -6 to 6
- targets: bfloat16 [2, 4, 896, 2048], P(None, None, 'dp'), may hold values from -6 to 6
- weights: bfloat16 [8, 2, 2, 96, 128, 128], P('section'), as said below
- pattern: int32 [8, 2, 2, 96, 2], P('section'), may hold values from 0 to 63, as said below
- master: float32 [8, 2, 96, 128, 128], P('section', None, None, 'dp'), may hold values from -0.6 to 0.6
- moment: float32 [8, 2, 96, 128, 128], P('section', None, None, 'dp'), as said below
- variance: float32 [8, 2, 96, 128, 128], P('section', None, None, 'dp'), as said below
Outputs:
- adam_step: float32 [8, 2, 96, 128, 128], P('section', None, None, 'dp')
- new_master: float32 [8, 2, 96, 128, 128], P('section', None, None, 'dp')
The draws below stay inside these ranges and needn't reach their ends.
Inputs may be any that keep to these rules, and one draw needn't show every extreme that they name: Within one layer and projection the 96 blocks are distinct and sorted; every block column of the up projection and every block row of the down projection holds one or more blocks. pattern[s,1] equals pattern[7 - s, 0]. Up blocks have rows below 16 and columns below 64, down blocks the reverse. weights[s,1] equals weights[7 - s, 0]; entries are scaled by the inverse root of the mean number of inputs per output. `moment`: of the order of the gradient. `variance`: Positive, of the order of the squared gradient.
All inputs are finite; a program needn't handle non-finite values.
Results may differ from the reference program's by a relative error of at most 0.022.
Values may be sent and summed in bfloat16 or wider, within the bound.
A program may use at most 192 MiB of HBM per device.

```python
import math
import jax
import jax.numpy as jnp
from jax import lax

D = 2048
FF = 8192
BS = 128
NNZ = 96
MICRO = 4
LAYERS = 8
REPLICA_ROWS = 896
TOTAL = 7168


def pick_blocks(seed_key, grid_rows, grid_cols, by_column):
    first_key, second_key = jax.random.split(seed_key)
    cell_count = grid_rows * grid_cols
    priority = jax.random.permutation(first_key, cell_count).astype(jnp.int32)
    if by_column:
        chosen = jax.random.randint(second_key, (grid_cols,), 0, grid_rows).astype(jnp.int32)
        forced = chosen * grid_cols + jnp.arange(grid_cols, dtype=jnp.int32)
    else:
        chosen = jax.random.randint(second_key, (grid_rows,), 0, grid_cols).astype(jnp.int32)
        forced = jnp.arange(grid_rows, dtype=jnp.int32) * grid_cols + chosen
    priority = priority.at[forced].add(cell_count)
    ignored, picked = lax.top_k(priority, NNZ)
    picked = jnp.sort(picked.astype(jnp.int32))
    return jnp.stack([picked // grid_cols, picked % grid_cols], axis=-1).astype(jnp.int32)


def draw_pattern(key, part):
    up_keys = jax.random.split(jax.random.fold_in(key, 11), LAYERS)
    down_keys = jax.random.split(jax.random.fold_in(key, 12), LAYERS)
    up_blocks = jax.vmap(lambda layer_key: pick_blocks(layer_key, D // BS, FF // BS, True))(up_keys)
    down_blocks = jax.vmap(lambda layer_key: pick_blocks(layer_key, FF // BS, D // BS, False))(down_keys)
    single = jnp.stack([up_blocks, down_blocks], axis=1)
    return jnp.stack([single, single[::-1]], axis=1)


def draw_weights(key, part):
    up_fan = BS * max(1.0, NNZ * BS / FF)
    down_fan = BS * max(1.0, NNZ * BS / D)
    single = jax.random.truncated_normal(jax.random.fold_in(key, 21), -4.0, 4.0, (LAYERS, 2, NNZ, BS, BS), jnp.float32)
    scales = jnp.array([up_fan ** (-0.5), down_fan ** (-0.5)], jnp.float32).reshape(1, 2, 1, 1, 1)
    single = single * scales
    return jnp.stack([single, single[::-1]], axis=1).astype(jnp.bfloat16)


def draw_moment(key, part):
    spread = 0.2 / math.sqrt(TOTAL)
    return (jax.random.normal(jax.random.fold_in(key, 31), (LAYERS, 2, NNZ, BS, BS), jnp.float32) * spread).astype(jnp.float32)


def draw_variance(key, part):
    lowest = math.log(0.01 / TOTAL)
    highest = math.log(0.1 / TOTAL)
    exponent = jax.random.uniform(jax.random.fold_in(key, 41), (LAYERS, 2, NNZ, BS, BS), jnp.float32, lowest, highest)
    return jnp.exp(exponent).astype(jnp.float32)


def block_scale(stream_key, dims, shards, smallest, top_value):
    def one(position, shards_of):
        steps = jax.random.uniform(jax.random.fold_in(jax.random.fold_in(stream_key, 6), position), (shards_of,), jnp.float32, smallest / len(shards), top_value / len(shards))
        return jnp.repeat(jnp.exp(steps), dims[position] // shards_of).reshape((-1,) + (1,) * (len(dims) - position - 1))

    loudness = one(*shards[0])
    for cut in shards[1:]:
        loudness = loudness * one(*cut)
    return loudness


def bell_draw(stream_key, dims, scale, limit, pieces=(), kind=jnp.bfloat16):
    values = jax.random.normal(stream_key, dims, jnp.float32) * scale
    if len(pieces) > 0:
        values = block_scale(stream_key, dims, pieces, -0.22, 0.18) * values
    return jnp.clip(values, min=-limit, max=limit).astype(kind)


def setup_inputs(seed: int = 0) -> dict:
    arg_keys = jax.random.split(jax.random.key(seed), 8)
    tokens = bell_draw(arg_keys[0], (2, MICRO, REPLICA_ROWS, D), 1.0, 6.0, ((2, 16),))
    targets = bell_draw(arg_keys[1], (2, MICRO, REPLICA_ROWS, D), 1.0, 6.0, ((2, 16),))
    weights = draw_weights(jax.random.fold_in(arg_keys[7], 71), 0)
    pattern = draw_pattern(jax.random.fold_in(arg_keys[7], 71), 0)
    master = bell_draw(arg_keys[4], (LAYERS, 2, NNZ, BS, BS), 0.1, 0.6, ((0, 8), (3, 16)), jnp.float32)
    moment = draw_moment(jax.random.fold_in(arg_keys[7], 71), 0)
    variance = draw_variance(jax.random.fold_in(arg_keys[7], 71), 0)
    return dict(tokens=tokens, targets=targets, weights=weights, pattern=pattern, master=master, moment=moment, variance=variance)


norm_eps = 1e-06
gelu_coef = 0.7978845608028654
beta_first = 0.9
beta_second = 0.95
adam_eps = 1e-08
learn_rate = 0.001
decay_rate = 0.1
update_count = 10

def sparse_product(left_rows, blocks, take_index, put_index, out_blocks):
    row_count = left_rows.shape[0]
    picked = jnp.take(left_rows.reshape(row_count, -1, BS), take_index, axis=1)
    product = jnp.einsum('rka,kab->krb', picked.astype(jnp.float32), blocks.astype(jnp.float32))
    summed = jax.ops.segment_sum(product, put_index, num_segments=out_blocks)
    return summed.transpose(1, 0, 2).reshape(row_count, out_blocks * BS)

def sparse_transposed(left_rows, blocks, take_index, put_index, out_blocks):
    row_count = left_rows.shape[0]
    picked = jnp.take(left_rows.reshape(row_count, -1, BS), take_index, axis=1)
    product = jnp.einsum('rkb,kab->kra', picked.astype(jnp.float32), blocks.astype(jnp.float32))
    summed = jax.ops.segment_sum(product, put_index, num_segments=out_blocks)
    return summed.transpose(1, 0, 2).reshape(row_count, out_blocks * BS)

def gelu_slope(preact):
    tanh_input = gelu_coef * (preact + 0.044715 * preact ** 3)
    tangent = jnp.tanh(tanh_input)
    return 0.5 * (1.0 + tangent) + 0.5 * preact * (1.0 - tangent * tangent) * gelu_coef * (1.0 + 3.0 * 0.044715 * preact * preact)

def layer_forward(inputs, layer_weights, layer_pattern):
    widened = inputs.astype(jnp.float32)
    factor = lax.rsqrt(lax.optimization_barrier(jnp.mean(widened * widened, axis=-1, keepdims=True)) + norm_eps)
    normed = (widened * factor).astype(jnp.bfloat16)
    preact = sparse_product(normed, layer_weights[0], layer_pattern[0, :, 0], layer_pattern[0, :, 1], FF // BS)
    hidden = jax.nn.gelu(preact, approximate=True).astype(jnp.bfloat16)
    mixed = sparse_product(hidden, layer_weights[1], layer_pattern[1, :, 0], layer_pattern[1, :, 1], D // BS)
    result = (widened + mixed).astype(jnp.bfloat16)
    return (result, normed, preact, hidden)

def layer_backward(inputs, preact, upstream, layer_weights, layer_pattern):
    grad_hidden = sparse_transposed(upstream, layer_weights[1], layer_pattern[1, :, 1], layer_pattern[1, :, 0], FF // BS)
    grad_preact = (grad_hidden * gelu_slope(preact)).astype(jnp.bfloat16)
    grad_normed = sparse_transposed(grad_preact, layer_weights[0], layer_pattern[0, :, 1], layer_pattern[0, :, 0], D // BS)
    widened = inputs.astype(jnp.float32)
    factor = lax.rsqrt(lax.optimization_barrier(jnp.mean(widened * widened, axis=-1, keepdims=True)) + norm_eps)
    coupling = lax.optimization_barrier(jnp.mean(widened * grad_normed, axis=-1, keepdims=True))
    downstream = upstream.astype(jnp.float32) + factor * grad_normed - widened * factor ** 3 * coupling
    return (downstream.astype(jnp.bfloat16), grad_preact)

def block_pairs(left_rows, right_rows, left_index, right_index):
    row_count = left_rows.shape[0]
    left_picked = jnp.take(left_rows.reshape(row_count, -1, BS), left_index, axis=1)
    right_picked = jnp.take(right_rows.reshape(row_count, -1, BS), right_index, axis=1)
    return jnp.einsum('rka,rkb->kab', left_picked.astype(jnp.float32), right_picked.astype(jnp.float32))

def weight_grads(normed, grad_preact, hidden, upstream, layer_pattern):
    up_part = block_pairs(normed, grad_preact, layer_pattern[0, :, 0], layer_pattern[0, :, 1])
    down_part = block_pairs(hidden, upstream, layer_pattern[1, :, 0], layer_pattern[1, :, 1])
    return jnp.stack([up_part, down_part])

def adam_update(grad_sum, master, moment, variance, token_total):
    gradient = grad_sum / token_total
    moment_next = beta_first * moment + (1.0 - beta_first) * gradient
    variance_next = beta_second * variance + (1.0 - beta_second) * gradient * gradient
    corrected = moment_next / (1.0 - beta_first ** update_count)
    spread = jnp.sqrt(variance_next / (1.0 - beta_second ** update_count))
    step_direction = corrected / (spread + adam_eps)
    return (step_direction, master - learn_rate * (step_direction + decay_rate * master))

def reference(tokens, targets, weights, pattern, master, moment, variance):
    layer_count = weights.shape[0]
    grad_list = [jnp.zeros((2, NNZ, BS, BS), jnp.float32) for layer_index in range(layer_count)]
    for stream in range(2):
        for micro_index in range(MICRO):
            current = tokens[stream, micro_index]
            history = []
            for layer_index in range(layer_count):
                result, normed, preact, hidden = layer_forward(current, weights[layer_index, 0], pattern[layer_index, 0])
                history.append((current, normed, preact, hidden))
                current = result
            upstream = (current.astype(jnp.float32) - targets[stream, micro_index].astype(jnp.float32)).astype(jnp.bfloat16)
            for layer_index in reversed(range(layer_count)):
                inputs, normed, preact, hidden = history[layer_index]
                downstream, grad_preact = layer_backward(inputs, preact, upstream, weights[layer_index, 0], pattern[layer_index, 0])
                grad_list[layer_index] = grad_list[layer_index] + weight_grads(normed, grad_preact, hidden, upstream, pattern[layer_index, 0])
                upstream = downstream
    token_total = 2 * MICRO * tokens.shape[2]
    grad_sum = jnp.stack(grad_list)
    return adam_update(grad_sum, master, moment, variance, token_total)
```

```python
import functools

import jax
import jax.numpy as jnp
from jax import lax
from jax.experimental import pallas as pl
from jax.experimental.pallas import tpu as pltpu
from jax.sharding import PartitionSpec as P

D = 2048
FF = 8192
BS = 128
NNZ = 96
DB = D // BS
FB = FF // BS
STAGES = 4
ROWS = 32
UNROLL = 48

norm_eps = 1e-06
gelu_coef = 0.7978845608028654
beta_first = 0.9
beta_second = 0.95
adam_eps = 1e-08
learn_rate = 0.001
decay_rate = 0.1
update_count = 10

MESH = pl.DeviceIdType.MESH
f32 = jnp.float32
bf16 = jnp.bfloat16

UPF_ROW, UPF_PERM, UP_LAST = 0, 96, 192
DNF_ROW, DNF_PERM, DN_LAST = 256, 352, 448
VB_COL, VB_LAST = 464, 560
UB_COL, UB_LAST = 624, 720
U_ROW, V_ROW = 736, 832
TABLE = 928
K_UPF, K_DNF, K_VB, K_UB, KEEPS = 0, 96, 192, 288, 384


def make_orders(chunks, cost_forward, cost_backward, hop):
    arrival = {(0, 0, c): 0.0 for c in range(chunks)}
    free = [0.0] * STAGES
    orders = [[] for _ in range(STAGES)]
    for _ in range(4 * STAGES * chunks):
        start, later, chunk, stage = min(
            (max(t, free[s]), -op, c, s) for (s, op, c), t in arrival.items()
        )
        op = -later
        del arrival[(stage, op, chunk)]
        end = start + (cost_forward if op < 2 else cost_backward)
        free[stage] = end
        orders[stage].append(op * chunks + chunk)
        following = stage + (1 if op % 2 == 0 else -1)
        if 0 <= following < STAGES:
            arrival[(following, op, chunk)] = end + hop
        elif op < 3:
            arrival[(stage, op + 1, chunk)] = end
    return orders


def tables(pattern):
    rows, cols = pattern[..., 0], pattern[..., 1]
    key = cols * 64 + rows
    rank = jnp.sum((key[..., None, :] < key[..., :, None]).astype(jnp.int32), axis=-1)
    slots = jnp.arange(NNZ, dtype=jnp.int32)
    hit = (rank[..., None, :] == slots[:, None]).astype(jnp.int32)
    perm = jnp.sum(hit * slots, axis=-1)
    sorted_rows = jnp.sum(hit * rows[..., None, :], axis=-1)
    sorted_cols = jnp.sum(hit * cols[..., None, :], axis=-1)

    def last(values, count):
        bins = jnp.arange(count, dtype=jnp.int32)[:, None]
        through = jnp.sum((values[..., None, :] <= bins).astype(jnp.int32), axis=-1)
        here = jnp.sum((values[..., None, :] == bins).astype(jnp.int32), axis=-1)
        return jnp.where(here > 0, through - 1, NNZ)

    def keep(values):
        same = (values[..., 1:] == values[..., :-1]).astype(f32)
        return jnp.concatenate([jnp.zeros_like(same[..., :1]), same], axis=-1)

    index = jnp.concatenate(
        [
            sorted_rows[:, 0],
            perm[:, 0],
            last(cols[:, 0], FB),
            sorted_rows[:, 1],
            perm[:, 1],
            last(cols[:, 1], DB),
            cols[:, 1],
            last(rows[:, 1], FB),
            cols[:, 0],
            last(rows[:, 0], DB),
            rows[:, 0],
            rows[:, 1],
        ],
        axis=-1,
    )
    keeps = jnp.concatenate(
        [keep(sorted_cols[:, 0]), keep(sorted_cols[:, 1]), keep(rows[:, 1]), keep(rows[:, 0])],
        axis=-1,
    )
    return index.reshape(-1), keeps.reshape(-1)


def pick(stage, values):
    out = jnp.int32(values[0])
    for s in range(1, STAGES):
        out = jnp.where(stage == s, jnp.int32(values[s]), out)
    return out


def pipeline_kernel(
    chunks,
    orders,
    tab,
    keeps,
    tok,
    tgt,
    wts,
    grads,
    W,
    WT,
    ACT,
    OUT,
    COT,
    NORM,
    H,
    S,
    TG,
    PS,
    w_sem,
    t_sem,
    send_sem,
    recv_sem,
):
    R = ROWS
    total_rows = chunks * R
    section = lax.axis_index("section")
    dp = lax.axis_index("dp")
    x, z_hi = section // 2, section % 2
    stage = jnp.where(section < 4, section, 7 - section)
    own = jnp.where(section < 4, 0, 1)

    def section_of(s):
        return jnp.where(s % 2 == z_hi, s, 7 - s)

    upper = section_of(stage + 1)
    lower = section_of(stage - 1)

    barrier = pltpu.get_barrier_semaphore()

    @pl.when(stage < STAGES - 1)
    def _():
        pl.semaphore_signal(barrier, inc=1, device_id=(upper, dp), device_id_type=MESH)

    @pl.when(stage > 0)
    def _():
        pl.semaphore_signal(barrier, inc=1, device_id=(lower, dp), device_id_type=MESH)

    def weight_copy(layer, proj):
        copy = own if layer == 0 else 1 - own
        return pltpu.make_async_copy(wts.at[copy, proj], W.at[layer, proj], w_sem.at[layer, proj])

    for layer in range(2):
        for proj in range(2):
            weight_copy(layer, proj).start()

    token_copy = pltpu.make_async_copy(tok, ACT.at[0], t_sem.at[0])
    target_copy = pltpu.make_async_copy(tgt, TG, t_sem.at[1])

    @pl.when(stage == 0)
    def _():
        token_copy.start()
        target_copy.start()

    PS[NNZ] = jnp.zeros((R, BS), f32)

    pl.semaphore_wait(barrier, jnp.where((stage == 0) | (stage == STAGES - 1), 1, 2))

    for layer in range(2):
        for proj in range(2):
            weight_copy(layer, proj).wait()

    @pl.when(stage == 0)
    def _():
        token_copy.wait()
        target_copy.wait()

    def link(op, chunk, target):
        rows = pl.ds(pl.multiple_of(chunk * R, R), R)
        return pltpu.make_async_remote_copy(
            src_ref=OUT.at[op, :, rows, :],
            dst_ref=ACT.at[op, :, rows, :],
            send_sem=send_sem.at[op, chunk],
            recv_sem=recv_sem.at[op, chunk],
            device_id=(target, dp),
            device_id_type=MESH,
        )

    def chain(keep_base, lhs, block):
        def step(outer, acc):
            first = outer * UNROLL
            products = [
                jnp.dot(lhs(first + u), block(first + u), preferred_element_type=f32)
                for u in range(UNROLL)
            ]
            sums = []
            for u in range(UNROLL):
                acc = acc * keeps[keep_base + first + u] + products[u]
                sums.append(acc)
            for u in range(UNROLL):
                PS[first + u] = sums[u]
            return acc

        lax.fori_loop(0, NNZ // UNROLL, step, jnp.zeros((R, BS), f32))

    def transpose_weights():
        def step(outer, c):
            for layer in range(2):
                for proj in range(2):
                    turned = [W[layer, proj, outer * 8 + u].T for u in range(8)]
                    for u in range(8):
                        WT[layer, proj, outer * 8 + u] = turned[u]
            return c

        lax.fori_loop(0, NNZ // 8, step, 0)

    def item(i, carry):
        code = jnp.int32(0)
        for t in range(len(orders[0])):
            code = jnp.where(i == t, pick(stage, [o[t] for o in orders]), code)
        op, chunk = code // chunks, code % chunks
        layer = jnp.where((op == 1) | (op == 2), 1, 0)
        copy = jnp.where(layer == 0, own, 1 - own)
        base = copy * TABLE
        keep_base = copy * KEEPS
        rows = pl.ds(pl.multiple_of(chunk * R, R), R)
        even = op % 2 == 0
        source = jnp.where(even, lower, upper)
        target = jnp.where(even, upper, lower)
        first = jnp.where(even, stage == 0, stage == STAGES - 1)
        final = jnp.where(even, stage == STAGES - 1, stage == 0)

        @pl.when(i == jnp.where(stage < 2, chunks, 0))
        def _():
            transpose_weights()

        @pl.when(jnp.logical_not(first))
        def _():
            link(op, chunk, source).wait_recv()

        def factor_of(act_op):
            def square(b, acc):
                v = ACT[act_op, b, rows, :].astype(f32)
                return acc + v * v

            total = lax.fori_loop(0, DB, square, jnp.zeros((R, BS), f32), unroll=True)
            return lax.rsqrt(jnp.sum(total, axis=-1, keepdims=True) * (1.0 / D) + norm_eps)

        @pl.when(op < 2)
        def _():
            factor = factor_of(op)

            def normalize(b, c):
                v = ACT[op, b, rows, :].astype(f32)
                NORM[layer, b, rows, :] = (v * factor).astype(bf16)
                return c

            lax.fori_loop(0, DB, normalize, 0, unroll=True)
            chain(
                keep_base + K_UPF,
                lambda k: NORM[layer, tab[base + UPF_ROW + k], rows, :],
                lambda k: W[layer, 0, tab[base + UPF_PERM + k]],
            )

            def activate(outer, c):
                results = []
                for u in range(16):
                    a = PS[tab[base + UP_LAST + outer * 16 + u]]
                    sq = a * a
                    th = jnp.tanh(a * (gelu_coef + (gelu_coef * 0.044715) * sq))
                    half = 0.5 + 0.5 * th
                    slope = half + (0.5 * a) * (1.0 - th * th) * (
                        gelu_coef + (gelu_coef * 3.0 * 0.044715) * sq
                    )
                    results.append(((a * half).astype(bf16), slope.astype(bf16)))
                for u in range(16):
                    H[layer, outer * 16 + u, rows, :] = results[u][0]
                    S[layer, outer * 16 + u, rows, :] = results[u][1]
                return c

            lax.fori_loop(0, FB // 16, activate, 0)
            chain(
                keep_base + K_DNF,
                lambda k: H[layer, tab[base + DNF_ROW + k], rows, :],
                lambda k: W[layer, 1, tab[base + DNF_PERM + k]],
            )

            def mixed(b):
                v = ACT[op, b, rows, :].astype(f32)
                return (v + PS[tab[base + DN_LAST + b]]).astype(bf16)

            @pl.when(jnp.logical_not(final))
            def _():
                def put(b, c):
                    OUT[op, b, rows, :] = mixed(b)
                    return c

                lax.fori_loop(0, DB, put, 0, unroll=True)

            @pl.when(jnp.logical_and(final, op == 0))
            def _():
                def put(b, c):
                    ACT[1, b, rows, :] = mixed(b)
                    return c

                lax.fori_loop(0, DB, put, 0, unroll=True)

            @pl.when(jnp.logical_and(final, op == 1))
            def _():
                def put(b, c):
                    residue = mixed(b).astype(f32) - TG[b, rows, :].astype(f32)
                    ACT[2, b, rows, :] = residue.astype(bf16)
                    return c

                lax.fori_loop(0, DB, put, 0, unroll=True)

        @pl.when(op >= 2)
        def _():
            inputs = 3 - op
            for b in range(DB):
                COT[layer, b, rows, :] = ACT[op, b, rows, :]
            chain(
                keep_base + K_VB,
                lambda k: COT[layer, tab[base + VB_COL + k], rows, :],
                lambda k: WT[layer, 1, k],
            )

            def slope_times(outer, c):
                results = []
                for u in range(16):
                    g = PS[tab[base + VB_LAST + outer * 16 + u]]
                    results.append(g * S[layer, outer * 16 + u, rows, :].astype(f32))
                for u in range(16):
                    S[layer, outer * 16 + u, rows, :] = results[u].astype(bf16)
                return c

            lax.fori_loop(0, FB // 16, slope_times, 0)

            @pl.when(jnp.logical_not(jnp.logical_and(final, op == 3)))
            def _():
                chain(
                    keep_base + K_UB,
                    lambda k: S[layer, tab[base + UB_COL + k], rows, :],
                    lambda k: WT[layer, 0, k],
                )
                factor = factor_of(inputs)

                def couple(b, acc):
                    v = ACT[inputs, b, rows, :].astype(f32)
                    return acc + v * PS[tab[base + UB_LAST + b]]

                coupling = lax.fori_loop(0, DB, couple, jnp.zeros((R, BS), f32), unroll=True)
                coupling = jnp.sum(coupling, axis=-1, keepdims=True) * (1.0 / D)
                pull = factor * factor * factor * coupling

                def downstream(b):
                    v = ACT[inputs, b, rows, :].astype(f32)
                    g = PS[tab[base + UB_LAST + b]]
                    return (ACT[op, b, rows, :].astype(f32) + factor * g - v * pull).astype(bf16)

                @pl.when(jnp.logical_not(final))
                def _():
                    def put(b, c):
                        OUT[op, b, rows, :] = downstream(b)
                        return c

                    lax.fori_loop(0, DB, put, 0, unroll=True)

                @pl.when(final)
                def _():
                    def put(b, c):
                        ACT[3, b, rows, :] = downstream(b)
                        return c

                    lax.fori_loop(0, DB, put, 0, unroll=True)

        @pl.when(jnp.logical_not(final))
        def _():
            link(op, chunk, target).start()

        return carry

    lax.fori_loop(0, 4 * chunks, item, 0)

    def pair(lhs, rhs):
        return lax.dot_general(lhs, rhs, (((0,), (0,)), ((), ())), preferred_element_type=f32)

    def weight_gradients(layer):
        base = jnp.where(own == layer, 0, TABLE)
        for proj in range(2):

            def blocks(outer, c, proj=proj):
                parts = []
                for u in range(16):
                    k = outer * 16 + u
                    if proj == 0:
                        lhs = NORM[layer, tab[base + U_ROW + k]]
                        rhs = S[layer, tab[base + UB_COL + k]]
                    else:
                        lhs = H[layer, tab[base + V_ROW + k]]
                        rhs = COT[layer, tab[base + VB_COL + k]]
                    parts.append(pair(lhs, rhs))
                for v in range(8):
                    for d in range(16):
                        both = jnp.concatenate(
                            [p[8 * d : 8 * d + 8] for p in parts[2 * v : 2 * v + 2]], axis=0
                        )
                        place = d * 12 + proj * 6 + outer
                        W[layer, place // NNZ, place % NNZ, 16 * v : 16 * v + 16, :] = both.astype(bf16)
                return c

            lax.fori_loop(0, NNZ // 16, blocks, 0)

    weight_gradients(1)
    weight_gradients(0)
    for layer in range(2):
        for half in range(2):
            copy = own if layer == 0 else 1 - own
            pltpu.make_async_copy(W.at[layer, half], grads.at[copy, half], w_sem.at[layer, half]).start()
    for layer in range(2):
        for half in range(2):
            copy = own if layer == 0 else 1 - own
            pltpu.make_async_copy(W.at[layer, half], grads.at[copy, half], w_sem.at[layer, half]).wait()

    def drain(i, carry):
        op, chunk = i // chunks, i % chunks
        even = op % 2 == 0
        target = jnp.where(even, upper, lower)
        final = jnp.where(even, stage == STAGES - 1, stage == 0)

        @pl.when(jnp.logical_not(final))
        def _():
            link(op, chunk, target).wait_send()

        return carry

    lax.fori_loop(0, 4 * chunks, drain, 0)


def adam_update(grad_sum, master, moment, variance, token_total):
    gradient = grad_sum / token_total
    moment_next = beta_first * moment + (1.0 - beta_first) * gradient
    variance_next = beta_second * variance + (1.0 - beta_second) * gradient * gradient
    corrected = moment_next / (1.0 - beta_first**update_count)
    spread = jnp.sqrt(variance_next / (1.0 - beta_second**update_count))
    step_direction = corrected / (spread + adam_eps)
    return (step_direction, master - learn_rate * (step_direction + decay_rate * master))


def shards(tokens, targets, weights, pattern, master, moment, variance):
    section = lax.axis_index("section")
    dp_size = lax.axis_size("dp")
    row_count = tokens.shape[1] * tokens.shape[2]
    chunks = row_count // ROWS

    def stream_rows(values):
        mine = lax.dynamic_index_in_dim(values, section % 2, 0, keepdims=False)
        return mine.reshape(row_count, DB, BS).transpose(1, 0, 2)

    index, keeps = tables(pattern[0])
    orders = make_orders(chunks, 1.7, 2.3, 3.0)
    smem = pl.BlockSpec(memory_space=pltpu.SMEM)
    anywhere = pl.BlockSpec(memory_space=pl.ANY)
    grads = pl.pallas_call(
        functools.partial(pipeline_kernel, chunks, orders),
        out_shape=jax.ShapeDtypeStruct((2, 2, NNZ, BS, BS), bf16),
        in_specs=[smem, smem, anywhere, anywhere, anywhere],
        out_specs=anywhere,
        scratch_shapes=[
            pltpu.VMEM((2, 2, NNZ, BS, BS), bf16),
            pltpu.VMEM((2, 2, NNZ, BS, BS), bf16),
            pltpu.VMEM((4, DB, row_count, BS), bf16),
            pltpu.VMEM((4, DB, row_count, BS), bf16),
            pltpu.VMEM((2, DB, row_count, BS), bf16),
            pltpu.VMEM((2, DB, row_count, BS), bf16),
            pltpu.VMEM((2, FB, row_count, BS), bf16),
            pltpu.VMEM((2, FB, row_count, BS), bf16),
            pltpu.VMEM((DB, row_count, BS), bf16),
            pltpu.VMEM((NNZ + 1, ROWS, BS), f32),
            pltpu.SemaphoreType.DMA((2, 2)),
            pltpu.SemaphoreType.DMA((2,)),
            pltpu.SemaphoreType.DMA((4, chunks)),
            pltpu.SemaphoreType.DMA((4, chunks)),
        ],
        compiler_params=pltpu.CompilerParams(
            collective_id=0, has_side_effects=True, vmem_limit_bytes=58 * 1024 * 1024
        ),
    )(index, keeps, stream_rows(tokens), stream_rows(targets), weights[0])

    grads = grads.reshape(2, 16, 2 * NNZ * 8, BS)
    shares = lax.psum_scatter(grads, "dp", scatter_dimension=1, tiled=True)
    shares = shares.reshape(2, 16 // dp_size, 2, NNZ, 8, BS).transpose(0, 2, 3, 1, 4, 5)
    shares = shares.reshape((2,) + master.shape[1:])
    sections = lax.axis_size("section")
    arrived = lax.ppermute(shares[1], "section", [(s, sections - 1 - s) for s in range(sections)])
    token_total = 2 * row_count * dp_size
    step_direction, master_next = adam_update(
        shares[0].astype(f32) + arrived.astype(f32), master[0], moment[0], variance[0], token_total
    )
    return (step_direction[None], master_next[None])


def solution(mesh):
    return jax.shard_map(
        shards,
        mesh=mesh,
        in_specs=(
            P(None, None, "dp", None),
            P(None, None, "dp", None),
            P("section", None, None, None, None, None),
            P("section", None, None, None, None),
            P("section", None, None, "dp", None),
            P("section", None, None, "dp", None),
            P("section", None, None, "dp", None),
        ),
        out_specs=(P("section", None, None, "dp", None), P("section", None, None, "dp", None)),
        check_vma=False,
    )
```

```python
import functools

import jax
import jax.numpy as jnp
from jax import lax
from jax.experimental import pallas as pl
from jax.experimental.pallas import tpu as pltpu
from jax.sharding import PartitionSpec as P

D = 2048
FF = 8192
BS = 128
NNZ = 96
DB = D // BS
FB = FF // BS
STAGES = 4
ROWS = 32
UNROLL = 48
STEPS = 6
SLICE = 6

norm_eps = 1e-06
gelu_coef = 0.7978845608028654
beta_first = 0.9
beta_second = 0.95
adam_eps = 1e-08
learn_rate = 0.001
decay_rate = 0.1
update_count = 10

MESH = pl.DeviceIdType.MESH
f32 = jnp.float32
bf16 = jnp.bfloat16

UPF_ROW, UPF_PERM, UP_LAST = 0, 96, 192
DNF_ROW, DNF_PERM, DN_LAST = 256, 352, 448
VB_COL, VB_LAST = 464, 560
UB_COL, UB_LAST = 624, 720
U_ROW, V_ROW = 736, 832
TABLE = 928
K_UPF, K_DNF, K_VB, K_UB, KEEPS = 0, 96, 192, 288, 384


def make_orders(chunks, cost_forward, cost_backward, hop):
    arrival = {(0, 0, c): 0.0 for c in range(chunks)}
    free = [0.0] * STAGES
    orders = [[] for _ in range(STAGES)]
    for _ in range(4 * STAGES * chunks):
        start, later, chunk, stage = min(
            (max(t, free[s]), -op, c, s) for (s, op, c), t in arrival.items()
        )
        op = -later
        del arrival[(stage, op, chunk)]
        end = start + (cost_forward if op < 2 else cost_backward)
        free[stage] = end
        orders[stage].append(op * chunks + chunk)
        following = stage + (1 if op % 2 == 0 else -1)
        if 0 <= following < STAGES:
            arrival[(following, op, chunk)] = end + hop
        elif op < 3:
            arrival[(stage, op + 1, chunk)] = end
    return orders


def make_sequences(chunks, orders):
    items = 4 * chunks
    sequences = []
    for order in orders:
        turn = order.index(2 * chunks + chunks - 1)
        code = lambda step, role: items + 2 * step + role
        first = [(turn, 0)] + [(turn + gap, step) for step, gap in ((1, 2), (2, 4), (3, 7))]
        placed = {}
        for at, step in first:
            if at < items and turn < items - 2:
                placed.setdefault(at, []).append(code(step, 1))
        sequence = []
        for n, item in enumerate(order):
            sequence.append(item)
            sequence.extend(placed.get(n, []))
        done = sum(len(v) for v in placed.values())
        early = [code(step, 1) for step in range(done, STEPS)]
        late = [code(step, 0) for step in range(STEPS)]
        if done == 0:
            sequence.append(early.pop(0))
        sequence.append(late.pop(0))
        while early or late:
            if early:
                sequence.append(early.pop(0))
            if late:
                sequence.append(late.pop(0))
        sequences.append(sequence)
    return sequences


def tables(pattern):
    rows, cols = pattern[..., 0], pattern[..., 1]
    key = cols * 64 + rows
    rank = jnp.sum((key[..., None, :] < key[..., :, None]).astype(jnp.int32), axis=-1)
    slots = jnp.arange(NNZ, dtype=jnp.int32)
    hit = (rank[..., None, :] == slots[:, None]).astype(jnp.int32)
    perm = jnp.sum(hit * slots, axis=-1)
    sorted_rows = jnp.sum(hit * rows[..., None, :], axis=-1)
    sorted_cols = jnp.sum(hit * cols[..., None, :], axis=-1)

    def last(values, count):
        bins = jnp.arange(count, dtype=jnp.int32)[:, None]
        through = jnp.sum((values[..., None, :] <= bins).astype(jnp.int32), axis=-1)
        here = jnp.sum((values[..., None, :] == bins).astype(jnp.int32), axis=-1)
        return jnp.where(here > 0, through - 1, NNZ)

    def keep(values):
        same = (values[..., 1:] == values[..., :-1]).astype(f32)
        return jnp.concatenate([jnp.zeros_like(same[..., :1]), same], axis=-1)

    index = jnp.concatenate(
        [
            sorted_rows[:, 0],
            perm[:, 0],
            last(cols[:, 0], FB),
            sorted_rows[:, 1],
            perm[:, 1],
            last(cols[:, 1], DB),
            cols[:, 1],
            last(rows[:, 1], FB),
            cols[:, 0],
            last(rows[:, 0], DB),
            rows[:, 0],
            rows[:, 1],
        ],
        axis=-1,
    )
    keeps = jnp.concatenate(
        [keep(sorted_cols[:, 0]), keep(sorted_cols[:, 1]), keep(rows[:, 1]), keep(rows[:, 0])],
        axis=-1,
    )
    return index.reshape(-1), keeps.reshape(-1)


def pick(stage, values):
    out = jnp.int32(values[0])
    for s in range(1, STAGES):
        out = jnp.where(stage == s, jnp.int32(values[s]), out)
    return out


def pipeline_kernel(
    chunks,
    sequences,
    tab,
    keeps,
    tok,
    tgt,
    wts,
    sums_out,
    W,
    WT,
    ACT,
    OUT,
    COT,
    NORM,
    H,
    S,
    TG,
    PS,
    w_sem,
    t_sem,
    send_sem,
    recv_sem,
    share_send,
    share_recv,
    ready_sem,
):
    R = ROWS
    total_rows = chunks * R
    section = lax.axis_index("section")
    dp = lax.axis_index("dp")
    x, z_hi = section // 2, section % 2
    stage = jnp.where(section < 4, section, 7 - section)
    own = jnp.where(section < 4, 0, 1)

    def section_of(s):
        return jnp.where(s % 2 == z_hi, s, 7 - s)

    upper = section_of(stage + 1)
    lower = section_of(stage - 1)

    core, z_lo, y = dp % 2, (dp // 2) % 2, dp // 4
    y_up, y_down, y_far = (y + 1) % 4, (y + 3) % 4, (y + 2) % 4
    peer_core = (section, dp + 1 - 2 * core)
    peer_up = (section, y_up * 4 + z_lo * 2 + core)
    peer_down = (section, y_down * 4 + z_lo * 2 + core)
    peer_z = (section, dp + 2 - 4 * z_lo)
    mirror = (7 - section, dp)
    peers = (peer_core, peer_up, peer_down, peer_z, mirror)

    barrier = pltpu.get_barrier_semaphore()

    @pl.when(stage < STAGES - 1)
    def _():
        pl.semaphore_signal(barrier, inc=1, device_id=(upper, dp), device_id_type=MESH)

    @pl.when(stage > 0)
    def _():
        pl.semaphore_signal(barrier, inc=1, device_id=(lower, dp), device_id_type=MESH)

    for peer in peers:
        pl.semaphore_signal(barrier, inc=1, device_id=peer, device_id_type=MESH)

    def weight_copy(layer, proj):
        copy = own if layer == 0 else 1 - own
        return pltpu.make_async_copy(wts.at[copy, proj], W.at[layer, proj], w_sem.at[layer, proj])

    for layer in range(2):
        for proj in range(2):
            weight_copy(layer, proj).start()

    token_copy = pltpu.make_async_copy(tok, ACT.at[0], t_sem.at[0])
    target_copy = pltpu.make_async_copy(tgt, TG, t_sem.at[1])

    @pl.when(stage == 0)
    def _():
        token_copy.start()
        target_copy.start()

    PS[NNZ] = jnp.zeros((R, BS), f32)

    pl.semaphore_wait(barrier, jnp.where((stage == 0) | (stage == STAGES - 1), 6, 7))

    for layer in range(2):
        for proj in range(2):
            weight_copy(layer, proj).wait()

    @pl.when(stage == 0)
    def _():
        token_copy.wait()
        target_copy.wait()

    def link(op, chunk, target):
        rows = pl.ds(pl.multiple_of(chunk * R, R), R)
        return pltpu.make_async_remote_copy(
            src_ref=OUT.at[op, :, rows, :],
            dst_ref=ACT.at[op, :, rows, :],
            send_sem=send_sem.at[op, chunk],
            recv_sem=recv_sem.at[op, chunk],
            device_id=(target, dp),
            device_id_type=MESH,
        )

    def chain(keep_base, lhs, block):
        def step(outer, acc):
            first = outer * UNROLL
            products = [
                jnp.dot(lhs(first + u), block(first + u), preferred_element_type=f32)
                for u in range(UNROLL)
            ]
            sums = []
            for u in range(UNROLL):
                acc = acc * keeps[keep_base + first + u] + products[u]
                sums.append(acc)
            for u in range(UNROLL):
                PS[first + u] = sums[u]
            return acc

        lax.fori_loop(0, NNZ // UNROLL, step, jnp.zeros((R, BS), f32))

    def transpose_weights():
        def step(outer, c):
            for layer in range(2):
                for proj in range(2):
                    turned = [W[layer, proj, outer * 8 + u].T for u in range(8)]
                    for u in range(8):
                        WT[layer, proj, outer * 8 + u] = turned[u]
            return c

        lax.fori_loop(0, NNZ // 8, step, 0)

    def item(code):
        op, chunk = code // chunks, code % chunks
        layer = jnp.where((op == 1) | (op == 2), 1, 0)
        copy = jnp.where(layer == 0, own, 1 - own)
        base = copy * TABLE
        keep_base = copy * KEEPS
        rows = pl.ds(pl.multiple_of(chunk * R, R), R)
        even = op % 2 == 0
        source = jnp.where(even, lower, upper)
        target = jnp.where(even, upper, lower)
        first = jnp.where(even, stage == 0, stage == STAGES - 1)
        final = jnp.where(even, stage == STAGES - 1, stage == 0)

        @pl.when(jnp.logical_not(first))
        def _():
            link(op, chunk, source).wait_recv()

        def factor_of(act_op):
            def square(b, acc):
                v = ACT[act_op, b, rows, :].astype(f32)
                return acc + v * v

            total = lax.fori_loop(0, DB, square, jnp.zeros((R, BS), f32), unroll=True)
            return lax.rsqrt(jnp.sum(total, axis=-1, keepdims=True) * (1.0 / D) + norm_eps)

        @pl.when(op < 2)
        def _():
            factor = factor_of(op)

            def normalize(b, c):
                v = ACT[op, b, rows, :].astype(f32)
                NORM[layer, b, rows, :] = (v * factor).astype(bf16)
                return c

            lax.fori_loop(0, DB, normalize, 0, unroll=True)
            chain(
                keep_base + K_UPF,
                lambda k: NORM[layer, tab[base + UPF_ROW + k], rows, :],
                lambda k: W[layer, 0, tab[base + UPF_PERM + k]],
            )

            def activate(outer, c):
                results = []
                for u in range(16):
                    a = PS[tab[base + UP_LAST + outer * 16 + u]]
                    sq = a * a
                    th = jnp.tanh(a * (gelu_coef + (gelu_coef * 0.044715) * sq))
                    half = 0.5 + 0.5 * th
                    slope = half + (0.5 * a) * (1.0 - th * th) * (
                        gelu_coef + (gelu_coef * 3.0 * 0.044715) * sq
                    )
                    results.append(((a * half).astype(bf16), slope.astype(bf16)))
                for u in range(16):
                    H[layer, outer * 16 + u, rows, :] = results[u][0]
                    S[layer, outer * 16 + u, rows, :] = results[u][1]
                return c

            lax.fori_loop(0, FB // 16, activate, 0)
            chain(
                keep_base + K_DNF,
                lambda k: H[layer, tab[base + DNF_ROW + k], rows, :],
                lambda k: W[layer, 1, tab[base + DNF_PERM + k]],
            )

            def mixed(b):
                v = ACT[op, b, rows, :].astype(f32)
                return (v + PS[tab[base + DN_LAST + b]]).astype(bf16)

            @pl.when(jnp.logical_not(final))
            def _():
                def put(b, c):
                    OUT[op, b, rows, :] = mixed(b)
                    return c

                lax.fori_loop(0, DB, put, 0, unroll=True)

            @pl.when(jnp.logical_and(final, op == 0))
            def _():
                def put(b, c):
                    ACT[1, b, rows, :] = mixed(b)
                    return c

                lax.fori_loop(0, DB, put, 0, unroll=True)

            @pl.when(jnp.logical_and(final, op == 1))
            def _():
                def put(b, c):
                    residue = mixed(b).astype(f32) - TG[b, rows, :].astype(f32)
                    ACT[2, b, rows, :] = residue.astype(bf16)
                    return c

                lax.fori_loop(0, DB, put, 0, unroll=True)

        @pl.when(op >= 2)
        def _():
            inputs = 3 - op
            for b in range(DB):
                COT[layer, b, rows, :] = ACT[op, b, rows, :]
            chain(
                keep_base + K_VB,
                lambda k: COT[layer, tab[base + VB_COL + k], rows, :],
                lambda k: WT[layer, 1, k],
            )

            def slope_times(outer, c):
                results = []
                for u in range(16):
                    g = PS[tab[base + VB_LAST + outer * 16 + u]]
                    results.append(g * S[layer, outer * 16 + u, rows, :].astype(f32))
                for u in range(16):
                    S[layer, outer * 16 + u, rows, :] = results[u].astype(bf16)
                return c

            lax.fori_loop(0, FB // 16, slope_times, 0)

            @pl.when(jnp.logical_not(jnp.logical_and(final, op == 3)))
            def _():
                chain(
                    keep_base + K_UB,
                    lambda k: S[layer, tab[base + UB_COL + k], rows, :],
                    lambda k: WT[layer, 0, k],
                )
                factor = factor_of(inputs)

                def couple(b, acc):
                    v = ACT[inputs, b, rows, :].astype(f32)
                    return acc + v * PS[tab[base + UB_LAST + b]]

                coupling = lax.fori_loop(0, DB, couple, jnp.zeros((R, BS), f32), unroll=True)
                coupling = jnp.sum(coupling, axis=-1, keepdims=True) * (1.0 / D)
                pull = factor * factor * factor * coupling

                def downstream(b):
                    v = ACT[inputs, b, rows, :].astype(f32)
                    g = PS[tab[base + UB_LAST + b]]
                    return (ACT[op, b, rows, :].astype(f32) + factor * g - v * pull).astype(bf16)

                @pl.when(jnp.logical_not(final))
                def _():
                    def put(b, c):
                        OUT[op, b, rows, :] = downstream(b)
                        return c

                    lax.fori_loop(0, DB, put, 0, unroll=True)

                @pl.when(final)
                def _():
                    def put(b, c):
                        ACT[3, b, rows, :] = downstream(b)
                        return c

                    lax.fori_loop(0, DB, put, 0, unroll=True)

        @pl.when(jnp.logical_not(final))
        def _():
            link(op, chunk, target).start()

    def pair(lhs, rhs):
        return lax.dot_general(lhs, rhs, (((0,), (0,)), ((), ())), preferred_element_type=f32)

    def weight_gradient(role, proj):
        base = jnp.where(role == 0, own, 1 - own) * TABLE

        def blocks(outer, c):
            parts = []
            for u in range(16):
                k = outer * 16 + u
                if proj == 0:
                    lhs = NORM[role, tab[base + U_ROW + k]]
                    rhs = S[role, tab[base + UB_COL + k]]
                else:
                    lhs = H[role, tab[base + V_ROW + k]]
                    rhs = COT[role, tab[base + VB_COL + k]]
                parts.append(pair(lhs, rhs))
            for v in range(8):
                for d in range(16):
                    both = jnp.concatenate(
                        [p[8 * d : 8 * d + 8] for p in parts[2 * v : 2 * v + 2]], axis=0
                    )
                    place = (d % 2) * 8 + (d // 4) * 2 + (d // 2) % 2
                    W[role, proj, place * SLICE + outer, 16 * v : 16 * v + 16, :] = both.astype(bf16)
            return c

        lax.fori_loop(0, NNZ // 16, blocks, 0)

    mine = core * 8 * SLICE

    def unit(of_y, of_z=0):
        return mine + (of_y * 2 + of_z) * SLICE

    def share_copy(role, proj, number):
        source, landing, count, peer = (
            ((1 - core) * 8 * SLICE, 0, 8 * SLICE, peer_core),
            (unit(y_far, 0), 48, SLICE, peer_up),
            (unit(y_far, 1), 54, SLICE, peer_down),
            (unit(y_up), 60, 2 * SLICE, peer_up),
            (unit(y_down), 72, 2 * SLICE, peer_down),
            (unit(y, 1 - z_lo), 84, SLICE, peer_z),
            (unit(y, z_lo), 90, SLICE, mirror),
        )[number]
        return pltpu.make_async_remote_copy(
            src_ref=W.at[role, proj, pl.ds(source, count)],
            dst_ref=WT.at[role, proj, pl.ds(landing, count)],
            send_sem=share_send.at[role, proj, number],
            recv_sem=share_recv.at[role, proj, number],
            device_id=peer,
            device_id_type=MESH,
        )

    def add(role, proj, place, landing, count):
        def step(n, c):
            there = WT[role, proj, landing + n].astype(f32)
            W[role, proj, place + n] = (W[role, proj, place + n].astype(f32) + there).astype(bf16)
            return c

        lax.fori_loop(0, count, step, 0, unroll=2)

    def add_two(role, proj, place, landing, other, count):
        def step(n, c):
            there = WT[role, proj, landing + n].astype(f32) + WT[role, proj, other + n].astype(f32)
            W[role, proj, place + n] = (W[role, proj, place + n].astype(f32) + there).astype(bf16)
            return c

        lax.fori_loop(0, count, step, 0, unroll=2)

    def action(code):
        step, role = (code - 4 * chunks) // 2, (code - 4 * chunks) % 2
        owner = own == role

        @pl.when(step == 0)
        def _():
            for number, peer in enumerate(peers[:4]):
                pl.semaphore_signal(ready_sem.at[role, number], inc=1, device_id=peer, device_id_type=MESH)

            @pl.when(owner)
            def _():
                pl.semaphore_signal(ready_sem.at[role, 4], inc=1, device_id=mirror, device_id_type=MESH)

            weight_gradient(role, 0)
            pl.semaphore_wait(ready_sem.at[role, 0], 1)
            share_copy(role, 0, 0).start()
            weight_gradient(role, 1)
            share_copy(role, 1, 0).start()

        @pl.when(step == 1)
        def _():
            for proj in range(2):
                share_copy(role, proj, 0).wait_recv()
                add(role, proj, mine, 0, 8 * SLICE)
                if proj == 0:
                    pl.semaphore_wait(ready_sem.at[role, 1], 1)
                    pl.semaphore_wait(ready_sem.at[role, 2], 1)
                share_copy(role, proj, 1).start()
                share_copy(role, proj, 2).start()

        @pl.when(step == 2)
        def _():
            for proj in range(2):
                share_copy(role, proj, 1).wait_recv()
                add(role, proj, unit(y_up, 0), 48, SLICE)
                share_copy(role, proj, 3).start()
                share_copy(role, proj, 2).wait_recv()
                add(role, proj, unit(y_down, 1), 54, SLICE)
                share_copy(role, proj, 4).start()

        @pl.when(step == 3)
        def _():
            for proj in range(2):
                share_copy(role, proj, 3).wait_recv()
                share_copy(role, proj, 4).wait_recv()
                add_two(role, proj, unit(y, 0), 60, 72, 2 * SLICE)
                if proj == 0:
                    pl.semaphore_wait(ready_sem.at[role, 3], 1)
                share_copy(role, proj, 5).start()

        @pl.when(step == 4)
        def _():
            for proj in range(2):
                share_copy(role, proj, 5).wait_recv()
                add(role, proj, unit(y, z_lo), 84, SLICE)

                @pl.when(jnp.logical_not(owner))
                def _(proj=proj):
                    if proj == 0:
                        pl.semaphore_wait(ready_sem.at[role, 4], 1)
                    share_copy(role, proj, 6).start()

        @pl.when(jnp.logical_and(step == 5, owner))
        def _():
            for proj in range(2):
                share_copy(role, proj, 6).wait_recv()

                def total(n, c, proj=proj):
                    there = WT[role, proj, 90 + n].astype(f32)
                    sums_out[proj, n] = W[role, proj, unit(y, z_lo) + n].astype(f32) + there
                    return c

                lax.fori_loop(0, SLICE, total, 0)

    def turn(i, carry):
        code = jnp.int32(0)
        for t in range(len(sequences[0])):
            code = jnp.where(i == t, pick(stage, [o[t] for o in sequences]), code)

        @pl.when(i == jnp.where(stage < 2, chunks, 0))
        def _():
            transpose_weights()

        @pl.when(code < 4 * chunks)
        def _():
            item(code)

        @pl.when(code >= 4 * chunks)
        def _():
            action(code)

        return carry

    lax.fori_loop(0, len(sequences[0]), turn, 0)

    def drain(i, carry):
        op, chunk = i // chunks, i % chunks
        even = op % 2 == 0
        target = jnp.where(even, upper, lower)
        final = jnp.where(even, stage == STAGES - 1, stage == 0)

        @pl.when(jnp.logical_not(final))
        def _():
            link(op, chunk, target).wait_send()

        return carry

    lax.fori_loop(0, 4 * chunks, drain, 0)
    for role in range(2):
        for proj in range(2):
            for number in range(6):
                share_copy(role, proj, number).wait_send()

            @pl.when(own != role)
            def _(role=role, proj=proj):
                share_copy(role, proj, 6).wait_send()


def adam_update(grad_sum, master, moment, variance, token_total):
    gradient = grad_sum / token_total
    moment_next = beta_first * moment + (1.0 - beta_first) * gradient
    variance_next = beta_second * variance + (1.0 - beta_second) * gradient * gradient
    corrected = moment_next / (1.0 - beta_first**update_count)
    spread = jnp.sqrt(variance_next / (1.0 - beta_second**update_count))
    step_direction = corrected / (spread + adam_eps)
    return (step_direction, master - learn_rate * (step_direction + decay_rate * master))


def shards(tokens, targets, weights, pattern, master, moment, variance):
    section = lax.axis_index("section")
    dp_size = lax.axis_size("dp")
    row_count = tokens.shape[1] * tokens.shape[2]
    chunks = row_count // ROWS

    def stream_rows(values):
        mine = lax.dynamic_index_in_dim(values, section % 2, 0, keepdims=False)
        return mine.reshape(row_count, DB, BS).transpose(1, 0, 2)

    index, keeps = tables(pattern[0])
    orders = make_orders(chunks, 1.7, 2.3, 3.0)
    smem = pl.BlockSpec(memory_space=pltpu.SMEM)
    anywhere = pl.BlockSpec(memory_space=pl.ANY)
    grads = pl.pallas_call(
        functools.partial(pipeline_kernel, chunks, make_sequences(chunks, orders)),
        out_shape=jax.ShapeDtypeStruct((2, SLICE, BS, BS), f32),
        in_specs=[smem, smem, anywhere, anywhere, anywhere],
        out_specs=pl.BlockSpec(memory_space=pltpu.VMEM),
        scratch_shapes=[
            pltpu.VMEM((2, 2, NNZ, BS, BS), bf16),
            pltpu.VMEM((2, 2, NNZ, BS, BS), bf16),
            pltpu.VMEM((4, DB, row_count, BS), bf16),
            pltpu.VMEM((4, DB, row_count, BS), bf16),
            pltpu.VMEM((2, DB, row_count, BS), bf16),
            pltpu.VMEM((2, DB, row_count, BS), bf16),
            pltpu.VMEM((2, FB, row_count, BS), bf16),
            pltpu.VMEM((2, FB, row_count, BS), bf16),
            pltpu.VMEM((DB, row_count, BS), bf16),
            pltpu.VMEM((NNZ + 1, ROWS, BS), f32),
            pltpu.SemaphoreType.DMA((2, 2)),
            pltpu.SemaphoreType.DMA((2,)),
            pltpu.SemaphoreType.DMA((4, chunks)),
            pltpu.SemaphoreType.DMA((4, chunks)),
            pltpu.SemaphoreType.DMA((2, 2, 7)),
            pltpu.SemaphoreType.DMA((2, 2, 7)),
            pltpu.SemaphoreType.REGULAR((2, 5)),
        ],
        compiler_params=pltpu.CompilerParams(
            collective_id=0, has_side_effects=True, vmem_limit_bytes=60 * 1024 * 1024
        ),
    )(index, keeps, stream_rows(tokens), stream_rows(targets), weights[0])

    token_total = 2 * row_count * dp_size
    step_direction, master_next = adam_update(
        grads.reshape(master.shape[1:]), master[0], moment[0], variance[0], token_total
    )
    return (step_direction[None], master_next[None])


def solution(mesh):
    return jax.shard_map(
        shards,
        mesh=mesh,
        in_specs=(
            P(None, None, "dp", None),
            P(None, None, "dp", None),
            P("section", None, None, None, None, None),
            P("section", None, None, None, None),
            P("section", None, None, "dp", None),
            P("section", None, None, "dp", None),
            P("section", None, None, "dp", None),
        ),
        out_specs=(P("section", None, None, "dp", None), P("section", None, None, "dp", None)),
        check_vma=False,
    )
```

```python
import functools

import jax
import jax.numpy as jnp
from jax import lax
from jax.experimental import pallas as pl
from jax.experimental.pallas import tpu as pltpu
from jax.sharding import PartitionSpec as P

D = 2048
FF = 8192
BS = 128
NNZ = 96
DB = D // BS
FB = FF // BS
STAGES = 4
ROWS = 32
STEPS = 7
SLICE = 6

norm_eps = 1e-06
gelu_coef = 0.7978845608028654
beta_first = 0.9
beta_second = 0.95
adam_eps = 1e-08
learn_rate = 0.001
decay_rate = 0.1
update_count = 10

MESH = pl.DeviceIdType.MESH
f32 = jnp.float32
bf16 = jnp.bfloat16

UPF_ROW, UPF_PERM, UP_LAST = 0, 96, 192
DNF_ROW, DNF_PERM, DN_LAST = 256, 352, 448
VB_COL, VB_LAST = 464, 560
UB_COL, UB_LAST = 624, 720
U_ROW, V_ROW = 736, 832
TABLE = 928
K_UPF, K_DNF, K_VB, K_UB, KEEPS = 0, 96, 192, 288, 384


def make_orders(chunks, cost_forward, cost_backward, hop):
    arrival = {(0, 0, c): 0.0 for c in range(chunks)}
    free = [0.0] * STAGES
    orders = [[] for _ in range(STAGES)]
    for _ in range(4 * STAGES * chunks):
        start, later, chunk, stage = min(
            (max(t, free[s]), -op, c, s) for (s, op, c), t in arrival.items()
        )
        op = -later
        del arrival[(stage, op, chunk)]
        end = start + (cost_forward if op < 2 else cost_backward)
        free[stage] = end
        orders[stage].append(op * chunks + chunk)
        following = stage + (1 if op % 2 == 0 else -1)
        if 0 <= following < STAGES:
            arrival[(following, op, chunk)] = end + hop
        elif op < 3:
            arrival[(stage, op + 1, chunk)] = end
    return orders


def make_sequences(chunks, orders):
    items = 4 * chunks
    sequences = []
    for order in orders:
        turn = order.index(2 * chunks + chunks - 1)
        code = lambda step, role: items + 2 * step + role
        first = [(turn, 0)] + [(turn + gap, step) for step, gap in ((1, 2), (2, 4), (3, 7))]
        placed = {}
        for at, step in first:
            if at < items - 1 and turn < items - 2:
                placed.setdefault(at, []).append(code(step, 1))
        sequence = []
        for n, item in enumerate(order):
            sequence.append(item)
            sequence.extend(placed.get(n, []))
        done = sum(len(v) for v in placed.values())
        early = [code(step, 1) for step in range(done, STEPS)]
        late = [code(step, 0) for step in range(STEPS)]
        if done == 0:
            sequence.append(early.pop(0))
        sequence.append(late.pop(0))
        while early or late:
            if early:
                sequence.append(early.pop(0))
            if late:
                sequence.append(late.pop(0))
        sequences.append(sequence)
    return sequences


def tables(pattern):
    rows, cols = pattern[..., 0], pattern[..., 1]
    key = cols * 64 + rows
    rank = jnp.sum((key[..., None, :] < key[..., :, None]).astype(jnp.int32), axis=-1)
    slots = jnp.arange(NNZ, dtype=jnp.int32)
    hit = (rank[..., None, :] == slots[:, None]).astype(jnp.int32)
    perm = jnp.sum(hit * slots, axis=-1)
    sorted_rows = jnp.sum(hit * rows[..., None, :], axis=-1)
    sorted_cols = jnp.sum(hit * cols[..., None, :], axis=-1)

    def last(values, count):
        bins = jnp.arange(count, dtype=jnp.int32)[:, None]
        through = jnp.sum((values[..., None, :] <= bins).astype(jnp.int32), axis=-1)
        here = jnp.sum((values[..., None, :] == bins).astype(jnp.int32), axis=-1)
        return jnp.where(here > 0, through - 1, NNZ)

    def keep(values):
        same = (values[..., 1:] == values[..., :-1]).astype(f32)
        return jnp.concatenate([jnp.zeros_like(same[..., :1]), same], axis=-1)

    index = jnp.concatenate(
        [
            sorted_rows[:, 0],
            perm[:, 0],
            last(cols[:, 0], FB),
            sorted_rows[:, 1],
            perm[:, 1],
            last(cols[:, 1], DB),
            cols[:, 1],
            last(rows[:, 1], FB),
            cols[:, 0],
            last(rows[:, 0], DB),
            rows[:, 0],
            rows[:, 1],
        ],
        axis=-1,
    )
    keeps = jnp.concatenate(
        [keep(sorted_cols[:, 0]), keep(sorted_cols[:, 1]), keep(rows[:, 1]), keep(rows[:, 0])],
        axis=-1,
    )
    return index.reshape(-1), keeps.reshape(-1)


def pick(stage, values):
    out = jnp.int32(values[0])
    for s in range(1, STAGES):
        out = jnp.where(stage == s, jnp.int32(values[s]), out)
    return out


def pipeline_kernel(
    chunks,
    sequences,
    tab,
    keeps,
    tok,
    tgt,
    wts,
    sums_out,
    W,
    WT,
    ACT,
    OUT,
    COT,
    NORM,
    H,
    S,
    TG,
    PS,
    w_sem,
    t_sem,
    send_sem,
    recv_sem,
    share_send,
    share_recv,
    ready_sem,
):
    R = ROWS
    total_rows = chunks * R
    section = lax.axis_index("section")
    dp = lax.axis_index("dp")
    z_hi = section % 2
    stage = jnp.where(section < 4, section, 7 - section)
    own = jnp.where(section < 4, 0, 1)

    core, z_lo, y = dp % 2, (dp // 2) % 2, dp // 4
    def section_of(s):
        return jnp.where(s % 2 == z_hi, s, 7 - s)

    upper = section_of(jnp.minimum(stage + 1, STAGES - 1))
    lower = section_of(jnp.maximum(stage - 1, 0))
    y_up, y_down, y_far = (y + 1) % 4, (y + 3) % 4, (y + 2) % 4
    peer_core = (section, dp + 1 - 2 * core)
    peer_up = (section, y_up * 4 + z_lo * 2 + core)
    peer_down = (section, y_down * 4 + z_lo * 2 + core)
    peer_z = (section, dp + 2 - 4 * z_lo)
    mirror = (7 - section, dp)
    peers = (peer_core, peer_up, peer_down, peer_z, mirror)

    barrier = pltpu.get_barrier_semaphore()

    @pl.when(stage < STAGES - 1)
    def _():
        pl.semaphore_signal(barrier, inc=1, device_id=(upper, dp), device_id_type=MESH)

    @pl.when(stage > 0)
    def _():
        pl.semaphore_signal(barrier, inc=1, device_id=(lower, dp), device_id_type=MESH)

    for peer in peers:
        pl.semaphore_signal(barrier, inc=1, device_id=peer, device_id_type=MESH)

    def weight_copy(layer, proj):
        copy = own if layer == 0 else 1 - own
        return pltpu.make_async_copy(wts.at[copy, proj], W.at[layer, proj], w_sem.at[layer, proj])

    for layer in range(2):
        for proj in range(2):
            weight_copy(layer, proj).start()

    def row_copies():
        for b in range(DB):
            columns = pl.ds(b * BS, BS)
            yield pltpu.make_async_copy(tok.at[z_hi, :, columns], ACT.at[0, b], t_sem.at[0, b])
        for b in range(DB):
            columns = pl.ds(b * BS, BS)
            yield pltpu.make_async_copy(tgt.at[z_hi, :, columns], TG.at[b], t_sem.at[1, b])

    @pl.when(stage == 0)
    def _():
        for copy in row_copies():
            copy.start()

    PS[NNZ] = jnp.zeros((R, BS), f32)

    pl.semaphore_wait(barrier, jnp.where((stage == 0) | (stage == STAGES - 1), 6, 7))

    for layer in range(2):
        for proj in range(2):
            weight_copy(layer, proj).wait()

    @pl.when(stage == 0)
    def _():
        for copy in row_copies():
            copy.wait()

    def link(op, chunk, target):
        rows = pl.ds(pl.multiple_of(chunk * R, R), R)
        return pltpu.make_async_remote_copy(
            src_ref=OUT.at[op, :, rows, :],
            dst_ref=ACT.at[op, :, rows, :],
            send_sem=send_sem.at[op, chunk],
            recv_sem=recv_sem.at[op, chunk],
            device_id=(target, dp),
            device_id_type=MESH,
        )

    def chain(keep_base, lhs, block, group=16, then=None):
        acc = jnp.zeros((R, BS), f32)
        done = 0
        for first in range(0, NNZ, group):
            slots = range(first, first + group)
            products = [jnp.dot(lhs(k), block(k), preferred_element_type=f32) for k in slots]
            stores = []
            if then is not None:
                ended = max(0, first - (NNZ - FB))
                stores = [then(j) for j in range(done, ended)]
                done = ended
            sums = []
            for u in range(group):
                acc = acc * keeps[keep_base + first + u] + products[u]
                sums.append(acc)
            for u in range(group):
                PS[first + u] = sums[u]
            for store in stores:
                store()
        if then is not None:
            for store in [then(j) for j in range(done, FB)]:
                store()

    def transpose_weights():
        def step(outer, c):
            for layer in range(2):
                for proj in range(2):
                    turned = [W[layer, proj, outer * 8 + u].T for u in range(8)]
                    for u in range(8):
                        WT[layer, proj, outer * 8 + u] = turned[u]
            return c

        lax.fori_loop(0, NNZ // 8, step, 0)

    def item(code):
        op, chunk = code // chunks, code % chunks
        layer = jnp.where((op == 1) | (op == 2), 1, 0)
        copy = jnp.where(layer == 0, own, 1 - own)
        base = copy * TABLE
        keep_base = copy * KEEPS
        rows = pl.ds(pl.multiple_of(chunk * R, R), R)
        even = op % 2 == 0
        source = jnp.where(even, lower, upper)
        target = jnp.where(even, upper, lower)
        first = jnp.where(even, stage == 0, stage == STAGES - 1)
        final = jnp.where(even, stage == STAGES - 1, stage == 0)

        @pl.when(jnp.logical_not(first))
        def _():
            link(op, chunk, source).wait_recv()

        def factor_of(act_op):
            def square(b, acc):
                v = ACT[act_op, b, rows, :].astype(f32)
                return acc + v * v

            total = lax.fori_loop(0, DB, square, jnp.zeros((R, BS), f32), unroll=True)
            return lax.rsqrt(jnp.sum(total, axis=-1, keepdims=True) * (1.0 / D) + norm_eps)

        @pl.when(op < 2)
        def _():
            factor = factor_of(op)

            def normalize(b, c):
                v = ACT[op, b, rows, :].astype(f32)
                NORM[layer, b, rows, :] = (v * factor).astype(bf16)
                return c

            lax.fori_loop(0, DB, normalize, 0, unroll=True)
            def activate(j):
                a = PS[tab[base + UP_LAST + j]]
                sq = a * a
                th = jnp.tanh(a * (gelu_coef + (gelu_coef * 0.044715) * sq))
                half = 0.5 + 0.5 * th
                slope = half + (0.5 * a) * (1.0 - th * th) * (
                    gelu_coef + (gelu_coef * 3.0 * 0.044715) * sq
                )
                hidden = (a * half).astype(bf16)
                slope = slope.astype(bf16)

                def store():
                    H[layer, j, rows, :] = hidden
                    S[layer, j, rows, :] = slope

                return store

            chain(
                keep_base + K_UPF,
                lambda k: NORM[layer, tab[base + UPF_ROW + k], rows, :],
                lambda k: W[layer, 0, tab[base + UPF_PERM + k]],
                group=8,
                then=activate,
            )
            chain(
                keep_base + K_DNF,
                lambda k: H[layer, tab[base + DNF_ROW + k], rows, :],
                lambda k: W[layer, 1, tab[base + DNF_PERM + k]],
            )

            def mixed(b):
                v = ACT[op, b, rows, :].astype(f32)
                return (v + PS[tab[base + DN_LAST + b]]).astype(bf16)

            @pl.when(jnp.logical_not(final))
            def _():
                def put(b, c):
                    OUT[op, b, rows, :] = mixed(b)
                    return c

                lax.fori_loop(0, DB, put, 0, unroll=True)

            @pl.when(jnp.logical_and(final, op == 0))
            def _():
                def put(b, c):
                    ACT[1, b, rows, :] = mixed(b)
                    return c

                lax.fori_loop(0, DB, put, 0, unroll=True)

            @pl.when(jnp.logical_and(final, op == 1))
            def _():
                def put(b, c):
                    residue = mixed(b).astype(f32) - TG[b, rows, :].astype(f32)
                    ACT[2, b, rows, :] = residue.astype(bf16)
                    return c

                lax.fori_loop(0, DB, put, 0, unroll=True)

        @pl.when(op >= 2)
        def _():
            inputs = 3 - op
            for b in range(DB):
                COT[layer, b, rows, :] = ACT[op, b, rows, :]
            def slope_times(j):
                g = PS[tab[base + VB_LAST + j]]
                result = (g * S[layer, j, rows, :].astype(f32)).astype(bf16)

                def store():
                    S[layer, j, rows, :] = result

                return store

            chain(
                keep_base + K_VB,
                lambda k: COT[layer, tab[base + VB_COL + k], rows, :],
                lambda k: WT[layer, 1, k],
                then=slope_times,
            )

            @pl.when(jnp.logical_not(jnp.logical_and(final, op == 3)))
            def _():
                chain(
                    keep_base + K_UB,
                    lambda k: S[layer, tab[base + UB_COL + k], rows, :],
                    lambda k: WT[layer, 0, k],
                )
                factor = factor_of(inputs)

                def couple(b, acc):
                    v = ACT[inputs, b, rows, :].astype(f32)
                    return acc + v * PS[tab[base + UB_LAST + b]]

                coupling = lax.fori_loop(0, DB, couple, jnp.zeros((R, BS), f32), unroll=True)
                coupling = jnp.sum(coupling, axis=-1, keepdims=True) * (1.0 / D)
                pull = factor * factor * factor * coupling

                def downstream(b):
                    v = ACT[inputs, b, rows, :].astype(f32)
                    g = PS[tab[base + UB_LAST + b]]
                    return (ACT[op, b, rows, :].astype(f32) + factor * g - v * pull).astype(bf16)

                @pl.when(jnp.logical_not(final))
                def _():
                    def put(b, c):
                        OUT[op, b, rows, :] = downstream(b)
                        return c

                    lax.fori_loop(0, DB, put, 0, unroll=True)

                @pl.when(final)
                def _():
                    def put(b, c):
                        ACT[3, b, rows, :] = downstream(b)
                        return c

                    lax.fori_loop(0, DB, put, 0, unroll=True)

        @pl.when(jnp.logical_not(final))
        def _():
            link(op, chunk, target).start()

    def pair(lhs, rhs):
        return lax.dot_general(lhs, rhs, (((0,), (0,)), ((), ())), preferred_element_type=f32)

    def weight_gradient(role, proj):
        base = jnp.where(role == 0, own, 1 - own) * TABLE

        def blocks(outer, c):
            parts = []
            for u in range(16):
                k = outer * 16 + u
                if proj == 0:
                    lhs = NORM[role, tab[base + U_ROW + k]]
                    rhs = S[role, tab[base + UB_COL + k]]
                else:
                    lhs = H[role, tab[base + V_ROW + k]]
                    rhs = COT[role, tab[base + VB_COL + k]]
                parts.append(pair(lhs, rhs))
            for v in range(8):
                for d in range(16):
                    both = jnp.concatenate(
                        [p[8 * d : 8 * d + 8] for p in parts[2 * v : 2 * v + 2]], axis=0
                    )
                    of_core, of_y, of_z = d % 2, d // 4, (d // 2) % 2
                    place = of_core * 8 + (of_y * 2 + of_z if proj == 0 else of_z * 4 + of_y)
                    W[role, proj, place * SLICE + outer, 16 * v : 16 * v + 16, :] = both.astype(bf16)
            return c

        lax.fori_loop(0, SLICE, blocks, 0)

    mine = core * 8 * SLICE

    def unit(proj, of_y, of_z):
        return mine + (of_y * 2 + of_z if proj == 0 else of_z * 4 + of_y) * SLICE

    CORE, FAR_UP, FAR_DOWN, UP, DOWN, Z, MIRROR = range(7)
    half = SLICE // 2
    copies = (
        (
            ((1 - core) * 8 * SLICE, 0, 48, peer_core),
            (unit(0, y_far, 0), 48, SLICE, peer_up),
            (unit(0, y_far, 1), 54, SLICE, peer_down),
            (unit(0, y_up, 0), 60, 2 * SLICE, peer_up),
            (unit(0, y_down, 0), 72, 2 * SLICE, peer_down),
            (unit(0, y, 1 - z_lo), 84, SLICE, peer_z),
            (unit(0, y, z_lo), 90, SLICE, mirror),
        ),
        (
            ((1 - core) * 8 * SLICE, 0, 48, peer_core),
            (unit(1, y_far, z_lo), 48, half, peer_up),
            (unit(1, y_far, z_lo) + half, 51, half, peer_down),
            (unit(1, y_up, z_lo), 54, SLICE, peer_up),
            (unit(1, y_down, z_lo), 60, SLICE, peer_down),
            (unit(1, 0, 1 - z_lo), 66, 4 * SLICE, peer_z),
            (unit(1, y, z_lo), 90, SLICE, mirror),
        ),
    )

    def share_copy(role, proj, number):
        source, landing, count, peer = copies[proj][number]
        return pltpu.make_async_remote_copy(
            src_ref=W.at[role, proj, pl.ds(source, count)],
            dst_ref=WT.at[role, proj, pl.ds(landing, count)],
            send_sem=share_send.at[role, proj, number],
            recv_sem=share_recv.at[role, proj, number],
            device_id=peer,
            device_id_type=MESH,
        )

    def add(role, proj, place, *numbers):
        for number in numbers:
            share_copy(role, proj, number).wait_recv()

        def step(n, c):
            total = W[role, proj, place + n].astype(f32)
            for number in numbers:
                total = total + WT[role, proj, copies[proj][number][1] + n].astype(f32)
            W[role, proj, place + n] = total.astype(bf16)
            return c

        lax.fori_loop(0, copies[proj][numbers[0]][2], step, 0, unroll=3)

    def send(role, proj, *numbers):
        for number in numbers:
            share_copy(role, proj, number).start()

    def action(code):
        step, role = (code - 4 * chunks) // 2, (code - 4 * chunks) % 2
        owner = own == role

        def wait_ready(number):
            pl.semaphore_wait(ready_sem.at[role, number], 1)

        def send_mirror(proj):
            @pl.when(jnp.logical_not(owner))
            def _():
                if proj == 0:
                    wait_ready(4)
                send(role, proj, MIRROR)

        @pl.when(step == 0)
        def _():
            for number, peer in enumerate(peers[:4]):
                pl.semaphore_signal(ready_sem.at[role, number], inc=1, device_id=peer, device_id_type=MESH)

            @pl.when(owner)
            def _():
                pl.semaphore_signal(ready_sem.at[role, 4], inc=1, device_id=mirror, device_id_type=MESH)

            weight_gradient(role, 1)
            wait_ready(0)
            send(role, 1, CORE)
            weight_gradient(role, 0)
            send(role, 0, CORE)

        @pl.when(step == 1)
        def _():
            add(role, 1, mine, CORE)
            wait_ready(3)
            send(role, 1, Z)
            add(role, 0, mine, CORE)
            wait_ready(1)
            wait_ready(2)
            send(role, 0, FAR_UP, FAR_DOWN)

        @pl.when(step == 2)
        def _():
            add(role, 0, unit(0, y_up, 0), FAR_UP)
            send(role, 0, UP)
            add(role, 0, unit(0, y_down, 1), FAR_DOWN)
            send(role, 0, DOWN)

        @pl.when(step == 3)
        def _():
            add(role, 0, unit(0, y, 0), UP, DOWN)
            send(role, 0, Z)
            add(role, 1, unit(1, 0, z_lo), Z)
            send(role, 1, FAR_UP, FAR_DOWN)

        @pl.when(step == 4)
        def _():
            add(role, 1, unit(1, y_up, z_lo), FAR_UP)
            send(role, 1, UP)
            add(role, 1, unit(1, y_down, z_lo) + half, FAR_DOWN)
            send(role, 1, DOWN)
            add(role, 0, unit(0, y, z_lo), Z)
            send_mirror(0)

        @pl.when(step == 5)
        def _():
            add(role, 1, unit(1, y, z_lo), UP, DOWN)
            send_mirror(1)

        @pl.when(jnp.logical_and(step == 6, owner))
        def _():
            for proj in range(2):
                share_copy(role, proj, MIRROR).wait_recv()
                for n in range(SLICE):
                    there = WT[role, proj, 90 + n].astype(f32)
                    sums_out[proj, n] = W[role, proj, unit(proj, y, z_lo) + n].astype(f32) + there

    def turn(i, carry):
        code = jnp.int32(0)
        for t in range(len(sequences[0])):
            code = jnp.where(i == t, pick(stage, [o[t] for o in sequences]), code)

        @pl.when(i == jnp.where(stage < 2, chunks, 0))
        def _():
            transpose_weights()

        @pl.when(code < 4 * chunks)
        def _():
            item(code)

        @pl.when(code >= 4 * chunks)
        def _():
            action(code)

        return carry

    lax.fori_loop(0, len(sequences[0]), turn, 0)

    def drain(i, carry):
        op, chunk = i // chunks, i % chunks
        even = op % 2 == 0
        target = jnp.where(even, upper, lower)
        final = jnp.where(even, stage == STAGES - 1, stage == 0)

        @pl.when(jnp.logical_not(final))
        def _():
            link(op, chunk, target).wait_send()

        return carry

    lax.fori_loop(0, 4 * chunks, drain, 0)
    for role in range(2):
        for proj in range(2):
            for number in range(MIRROR):
                share_copy(role, proj, number).wait_send()

            @pl.when(own != role)
            def _(role=role, proj=proj):
                share_copy(role, proj, MIRROR).wait_send()


def adam_update(grad_sum, master, moment, variance, token_total):
    gradient = grad_sum / token_total
    moment_next = beta_first * moment + (1.0 - beta_first) * gradient
    variance_next = beta_second * variance + (1.0 - beta_second) * gradient * gradient
    corrected = moment_next / (1.0 - beta_first**update_count)
    spread = jnp.sqrt(variance_next / (1.0 - beta_second**update_count))
    step_direction = corrected / (spread + adam_eps)
    return (step_direction, master - learn_rate * (step_direction + decay_rate * master))


def shards(tokens, targets, weights, pattern, master, moment, variance):
    dp_size = lax.axis_size("dp")
    row_count = tokens.shape[1] * tokens.shape[2]
    chunks = row_count // ROWS

    index, keeps = tables(pattern[0])
    orders = make_orders(chunks, 2.6, 2.5, 4.5)
    smem = pl.BlockSpec(memory_space=pltpu.SMEM)
    anywhere = pl.BlockSpec(memory_space=pl.ANY)
    grads = pl.pallas_call(
        functools.partial(pipeline_kernel, chunks, make_sequences(chunks, orders)),
        out_shape=jax.ShapeDtypeStruct((2, SLICE, BS, BS), f32),
        in_specs=[smem, smem, anywhere, anywhere, anywhere],
        out_specs=pl.BlockSpec(memory_space=pltpu.VMEM),
        scratch_shapes=[
            pltpu.VMEM((2, 2, NNZ, BS, BS), bf16),
            pltpu.VMEM((2, 2, NNZ, BS, BS), bf16),
            pltpu.VMEM((4, DB, row_count, BS), bf16),
            pltpu.VMEM((4, DB, row_count, BS), bf16),
            pltpu.VMEM((2, DB, row_count, BS), bf16),
            pltpu.VMEM((2, DB, row_count, BS), bf16),
            pltpu.VMEM((2, FB, row_count, BS), bf16),
            pltpu.VMEM((2, FB, row_count, BS), bf16),
            pltpu.VMEM((DB, row_count, BS), bf16),
            pltpu.VMEM((NNZ + 1, ROWS, BS), f32),
            pltpu.SemaphoreType.DMA((2, 2)),
            pltpu.SemaphoreType.DMA((2, DB)),
            pltpu.SemaphoreType.DMA((4, chunks)),
            pltpu.SemaphoreType.DMA((4, chunks)),
            pltpu.SemaphoreType.DMA((2, 2, 7)),
            pltpu.SemaphoreType.DMA((2, 2, 7)),
            pltpu.SemaphoreType.REGULAR((2, 5)),
        ],
        compiler_params=pltpu.CompilerParams(
            collective_id=0, has_side_effects=True, vmem_limit_bytes=60 * 1024 * 1024
        ),
    )(index, keeps, tokens.reshape(2, row_count, D), targets.reshape(2, row_count, D), weights[0])

    token_total = 2 * row_count * dp_size
    step_direction, master_next = adam_update(
        grads.reshape(master.shape[1:]), master[0], moment[0], variance[0], token_total
    )
    return (step_direction[None], master_next[None])


def solution(mesh):
    return jax.shard_map(
        shards,
        mesh=mesh,
        in_specs=(
            P(None, None, "dp", None),
            P(None, None, "dp", None),
            P("section", None, None, None, None, None),
            P("section", None, None, None, None),
            P("section", None, None, "dp", None),
            P("section", None, None, "dp", None),
            P("section", None, None, "dp", None),
        ),
        out_specs=(P("section", None, None, "dp", None), P("section", None, None, "dp", None)),
        check_vma=False,
    )
```

```python
import functools

import jax
import jax.numpy as jnp
from jax import lax
from jax.experimental import pallas as pl
from jax.experimental.pallas import tpu as pltpu
from jax.sharding import PartitionSpec as P

D = 2048
FF = 8192
BS = 128
NNZ = 96
DB = D // BS
FB = FF // BS
STAGES = 4
ROWS = 32
STEPS = 7
SLICE = 6

norm_eps = 1e-06
gelu_coef = 0.7978845608028654
beta_first = 0.9
beta_second = 0.95
adam_eps = 1e-08
learn_rate = 0.001
decay_rate = 0.1
update_count = 10

MESH = pl.DeviceIdType.MESH
f32 = jnp.float32
bf16 = jnp.bfloat16

UPF_ROW, UPF_PERM, UP_LAST = 0, 96, 192
DNF_ROW, DNF_PERM, DN_LAST = 256, 352, 448
VB_COL, VB_LAST = 464, 560
UB_COL, UB_LAST = 624, 720
U_ROW, V_ROW = 736, 832
TABLE = 928
K_UPF, K_DNF, K_VB, K_UB, KEEPS = 0, 96, 192, 288, 384


def make_orders(chunks, cost_forward, cost_backward, hop):
    arrival = {(0, 0, c): 0.0 for c in range(chunks)}
    free = [0.0] * STAGES
    orders = [[] for _ in range(STAGES)]
    for _ in range(4 * STAGES * chunks):
        start, later, chunk, stage = min(
            (max(t, free[s]), -op, c, s) for (s, op, c), t in arrival.items()
        )
        op = -later
        del arrival[(stage, op, chunk)]
        end = start + (cost_forward if op < 2 else cost_backward)
        free[stage] = end
        orders[stage].append(op * chunks + chunk)
        following = stage + (1 if op % 2 == 0 else -1)
        if 0 <= following < STAGES:
            arrival[(following, op, chunk)] = end + hop
        elif op < 3:
            arrival[(stage, op + 1, chunk)] = end
    return orders


def make_sequences(chunks, orders):
    items = 4 * chunks
    sequences = []
    for order in orders:
        turn = order.index(2 * chunks + chunks - 1)
        code = lambda step, role: items + 2 * step + role
        first = [(turn, 0)] + [(turn + gap, step) for step, gap in ((1, 2), (2, 3), (3, 6))]
        placed = {}
        for at, step in first:
            if at < items - 1 and turn < items - 2:
                placed.setdefault(at, []).append(code(step, 1))
        sequence = []
        for n, item in enumerate(order):
            sequence.append(item)
            sequence.extend(placed.get(n, []))
        done = sum(len(v) for v in placed.values())
        early = [code(step, 1) for step in range(done, STEPS)]
        late = [code(step, 0) for step in range(STEPS)]
        if done == 0:
            sequence.append(early.pop(0))
        sequence.append(late.pop(0))
        while early or late:
            if early:
                sequence.append(early.pop(0))
            if late:
                sequence.append(late.pop(0))
        sequences.append(sequence)
    return sequences


def tables(pattern):
    rows, cols = pattern[..., 0], pattern[..., 1]
    key = cols * 64 + rows
    rank = jnp.sum((key[..., None, :] < key[..., :, None]).astype(jnp.int32), axis=-1)
    slots = jnp.arange(NNZ, dtype=jnp.int32)
    hit = (rank[..., None, :] == slots[:, None]).astype(jnp.int32)
    perm = jnp.sum(hit * slots, axis=-1)
    sorted_rows = jnp.sum(hit * rows[..., None, :], axis=-1)
    sorted_cols = jnp.sum(hit * cols[..., None, :], axis=-1)

    def last(values, count):
        bins = jnp.arange(count, dtype=jnp.int32)[:, None]
        through = jnp.sum((values[..., None, :] <= bins).astype(jnp.int32), axis=-1)
        here = jnp.sum((values[..., None, :] == bins).astype(jnp.int32), axis=-1)
        return jnp.where(here > 0, through - 1, NNZ)

    def keep(values):
        same = (values[..., 1:] == values[..., :-1]).astype(f32)
        return jnp.concatenate([jnp.zeros_like(same[..., :1]), same], axis=-1)

    index = jnp.concatenate(
        [
            sorted_rows[:, 0],
            perm[:, 0],
            last(cols[:, 0], FB),
            sorted_rows[:, 1],
            perm[:, 1],
            last(cols[:, 1], DB),
            cols[:, 1],
            last(rows[:, 1], FB),
            cols[:, 0],
            last(rows[:, 0], DB),
            rows[:, 0],
            rows[:, 1],
        ],
        axis=-1,
    )
    keeps = jnp.concatenate(
        [keep(sorted_cols[:, 0]), keep(sorted_cols[:, 1]), keep(rows[:, 1]), keep(rows[:, 0])],
        axis=-1,
    )
    return index.reshape(-1), keeps.reshape(-1)


def pick(stage, values):
    out = jnp.int32(values[0])
    for s in range(1, STAGES):
        out = jnp.where(stage == s, jnp.int32(values[s]), out)
    return out


def pipeline_kernel(
    chunks,
    sequences,
    tab,
    keeps,
    tok,
    tgt,
    wts,
    sums_out,
    W,
    WT,
    ACT,
    OUT,
    COT,
    NORM,
    H,
    S,
    TG,
    PS,
    w_sem,
    t_sem,
    send_sem,
    recv_sem,
    share_send,
    share_recv,
    ready_sem,
):
    R = ROWS
    total_rows = chunks * R
    section = lax.axis_index("section")
    dp = lax.axis_index("dp")
    z_hi = section % 2
    stage = jnp.where(section < 4, section, 7 - section)
    own = jnp.where(section < 4, 0, 1)

    core, z_lo, y = dp % 2, (dp // 2) % 2, dp // 4
    def section_of(s):
        return jnp.where(s % 2 == z_hi, s, 7 - s)

    upper = section_of(jnp.minimum(stage + 1, STAGES - 1))
    lower = section_of(jnp.maximum(stage - 1, 0))
    y_up, y_down, y_far = (y + 1) % 4, (y + 3) % 4, (y + 2) % 4
    peer_core = (section, dp + 1 - 2 * core)
    peer_up = (section, y_up * 4 + z_lo * 2 + core)
    peer_down = (section, y_down * 4 + z_lo * 2 + core)
    peer_z = (section, dp + 2 - 4 * z_lo)
    mirror = (7 - section, dp)
    peers = (peer_core, peer_up, peer_down, peer_z, mirror)

    barrier = pltpu.get_barrier_semaphore()

    @pl.when(stage < STAGES - 1)
    def _():
        pl.semaphore_signal(barrier, inc=1, device_id=(upper, dp), device_id_type=MESH)

    @pl.when(stage > 0)
    def _():
        pl.semaphore_signal(barrier, inc=1, device_id=(lower, dp), device_id_type=MESH)

    for peer in peers:
        pl.semaphore_signal(barrier, inc=1, device_id=peer, device_id_type=MESH)

    def weight_copy(layer, proj):
        copy = own if layer == 0 else 1 - own
        return pltpu.make_async_copy(wts.at[copy, proj], W.at[layer, proj], w_sem.at[layer, proj])

    for layer in range(2):
        for proj in range(2):
            weight_copy(layer, proj).start()

    def row_copies():
        for b in range(DB):
            columns = pl.ds(b * BS, BS)
            yield pltpu.make_async_copy(tok.at[z_hi, :, columns], ACT.at[0, b], t_sem.at[0, b])
        for b in range(DB):
            columns = pl.ds(b * BS, BS)
            yield pltpu.make_async_copy(tgt.at[z_hi, :, columns], TG.at[b], t_sem.at[1, b])

    @pl.when(stage == 0)
    def _():
        for copy in row_copies():
            copy.start()

    PS[NNZ] = jnp.zeros((R, BS), f32)

    pl.semaphore_wait(barrier, jnp.where((stage == 0) | (stage == STAGES - 1), 6, 7))

    for layer in range(2):
        for proj in range(2):
            weight_copy(layer, proj).wait()

    @pl.when(stage == 0)
    def _():
        for copy in row_copies():
            copy.wait()

    def link(op, chunk, target):
        rows = pl.ds(pl.multiple_of(chunk * R, R), R)
        return pltpu.make_async_remote_copy(
            src_ref=OUT.at[op, :, rows, :],
            dst_ref=ACT.at[op, :, rows, :],
            send_sem=send_sem.at[op, chunk],
            recv_sem=recv_sem.at[op, chunk],
            device_id=(target, dp),
            device_id_type=MESH,
        )

    def chain(keep_base, lhs, block, group=16, then=None):
        acc = jnp.zeros((R, BS), f32)
        done = 0
        for first in range(0, NNZ, group):
            slots = range(first, first + group)
            products = [jnp.dot(lhs(k), block(k), preferred_element_type=f32) for k in slots]
            stores = []
            if then is not None:
                ended = max(0, first - (NNZ - FB))
                stores = [then(j) for j in range(done, ended)]
                done = ended
            sums = []
            for u in range(group):
                acc = acc * keeps[keep_base + first + u] + products[u]
                sums.append(acc)
            for u in range(group):
                PS[first + u] = sums[u]
            for store in stores:
                store()
        if then is not None:
            for store in [then(j) for j in range(done, FB)]:
                store()

    def transpose_weights():
        def step(outer, c):
            for layer in range(2):
                for proj in range(2):
                    turned = [W[layer, proj, outer * 8 + u].T for u in range(8)]
                    for u in range(8):
                        WT[layer, proj, outer * 8 + u] = turned[u]
            return c

        lax.fori_loop(0, NNZ // 8, step, 0)

    def item(code):
        op, chunk = code // chunks, code % chunks
        layer = jnp.where((op == 1) | (op == 2), 1, 0)
        copy = jnp.where(layer == 0, own, 1 - own)
        base = copy * TABLE
        keep_base = copy * KEEPS
        rows = pl.ds(pl.multiple_of(chunk * R, R), R)
        even = op % 2 == 0
        source = jnp.where(even, lower, upper)
        target = jnp.where(even, upper, lower)
        first = jnp.where(even, stage == 0, stage == STAGES - 1)
        final = jnp.where(even, stage == STAGES - 1, stage == 0)

        @pl.when(jnp.logical_not(first))
        def _():
            link(op, chunk, source).wait_recv()

        def factor_of(act_op):
            def square(b, acc):
                v = ACT[act_op, b, rows, :].astype(f32)
                return acc + v * v

            total = lax.fori_loop(0, DB, square, jnp.zeros((R, BS), f32), unroll=True)
            return lax.rsqrt(jnp.sum(total, axis=-1, keepdims=True) * (1.0 / D) + norm_eps)

        @pl.when(op < 2)
        def _():
            factor = factor_of(op)

            def normalize(b, c):
                v = ACT[op, b, rows, :].astype(f32)
                NORM[layer, b, rows, :] = (v * factor).astype(bf16)
                return c

            lax.fori_loop(0, DB, normalize, 0, unroll=True)
            def activate(j):
                a = PS[tab[base + UP_LAST + j]]
                sq = a * a
                th = jnp.tanh(a * (gelu_coef + (gelu_coef * 0.044715) * sq))
                half = 0.5 + 0.5 * th
                slope = half + (0.5 * a) * (1.0 - th * th) * (
                    gelu_coef + (gelu_coef * 3.0 * 0.044715) * sq
                )
                hidden = (a * half).astype(bf16)
                slope = slope.astype(bf16)

                def store():
                    H[layer, j, rows, :] = hidden
                    S[layer, j, rows, :] = slope

                return store

            chain(
                keep_base + K_UPF,
                lambda k: NORM[layer, tab[base + UPF_ROW + k], rows, :],
                lambda k: W[layer, 0, tab[base + UPF_PERM + k]],
                group=8,
                then=activate,
            )
            chain(
                keep_base + K_DNF,
                lambda k: H[layer, tab[base + DNF_ROW + k], rows, :],
                lambda k: W[layer, 1, tab[base + DNF_PERM + k]],
            )

            def mixed(b):
                v = ACT[op, b, rows, :].astype(f32)
                return (v + PS[tab[base + DN_LAST + b]]).astype(bf16)

            @pl.when(jnp.logical_not(final))
            def _():
                def put(b, c):
                    OUT[op, b, rows, :] = mixed(b)
                    return c

                lax.fori_loop(0, DB, put, 0, unroll=True)

            @pl.when(jnp.logical_and(final, op == 0))
            def _():
                def put(b, c):
                    ACT[1, b, rows, :] = mixed(b)
                    return c

                lax.fori_loop(0, DB, put, 0, unroll=True)

            @pl.when(jnp.logical_and(final, op == 1))
            def _():
                def put(b, c):
                    residue = mixed(b).astype(f32) - TG[b, rows, :].astype(f32)
                    ACT[2, b, rows, :] = residue.astype(bf16)
                    return c

                lax.fori_loop(0, DB, put, 0, unroll=True)

        @pl.when(op >= 2)
        def _():
            inputs = 3 - op
            for b in range(DB):
                COT[layer, b, rows, :] = ACT[op, b, rows, :]
            def slope_times(j):
                g = PS[tab[base + VB_LAST + j]]
                result = (g * S[layer, j, rows, :].astype(f32)).astype(bf16)

                def store():
                    S[layer, j, rows, :] = result

                return store

            chain(
                keep_base + K_VB,
                lambda k: COT[layer, tab[base + VB_COL + k], rows, :],
                lambda k: WT[layer, 1, k],
                then=slope_times,
            )

            @pl.when(jnp.logical_not(jnp.logical_and(final, op == 3)))
            def _():
                chain(
                    keep_base + K_UB,
                    lambda k: S[layer, tab[base + UB_COL + k], rows, :],
                    lambda k: WT[layer, 0, k],
                )
                factor = factor_of(inputs)

                def couple(b, acc):
                    v = ACT[inputs, b, rows, :].astype(f32)
                    return acc + v * PS[tab[base + UB_LAST + b]]

                coupling = lax.fori_loop(0, DB, couple, jnp.zeros((R, BS), f32), unroll=True)
                coupling = jnp.sum(coupling, axis=-1, keepdims=True) * (1.0 / D)
                pull = factor * factor * factor * coupling

                def downstream(b):
                    v = ACT[inputs, b, rows, :].astype(f32)
                    g = PS[tab[base + UB_LAST + b]]
                    return (ACT[op, b, rows, :].astype(f32) + factor * g - v * pull).astype(bf16)

                @pl.when(jnp.logical_not(final))
                def _():
                    def put(b, c):
                        OUT[op, b, rows, :] = downstream(b)
                        return c

                    lax.fori_loop(0, DB, put, 0, unroll=True)

                @pl.when(final)
                def _():
                    def put(b, c):
                        ACT[3, b, rows, :] = downstream(b)
                        return c

                    lax.fori_loop(0, DB, put, 0, unroll=True)

        @pl.when(jnp.logical_not(final))
        def _():
            link(op, chunk, target).start()

    def pair(lhs, rhs):
        return lax.dot_general(lhs, rhs, (((0,), (0,)), ((), ())), preferred_element_type=f32)

    def weight_gradient(role, proj):
        base = jnp.where(role == 0, own, 1 - own) * TABLE

        def blocks(outer, c):
            parts = []
            for u in range(16):
                k = outer * 16 + u
                if proj == 0:
                    lhs = NORM[role, tab[base + U_ROW + k]]
                    rhs = S[role, tab[base + UB_COL + k]]
                else:
                    lhs = H[role, tab[base + V_ROW + k]]
                    rhs = COT[role, tab[base + VB_COL + k]]
                parts.append(pair(lhs, rhs))
            for v in range(8):
                for d in range(16):
                    both = jnp.concatenate(
                        [p[8 * d : 8 * d + 8] for p in parts[2 * v : 2 * v + 2]], axis=0
                    )
                    of_core, of_y, of_z = d % 2, d // 4, (d // 2) % 2
                    place = of_core * 8 + (of_y * 2 + of_z if proj == 0 else of_z * 4 + of_y)
                    W[role, proj, place * SLICE + outer, 16 * v : 16 * v + 16, :] = both.astype(bf16)
            return c

        lax.fori_loop(0, SLICE, blocks, 0)

    mine = core * 8 * SLICE

    def unit(proj, of_y, of_z):
        return mine + (of_y * 2 + of_z if proj == 0 else of_z * 4 + of_y) * SLICE

    CORE, FAR_UP, FAR_DOWN, UP, DOWN, Z, MIRROR = range(7)
    half = SLICE // 2
    copies = (
        (
            ((1 - core) * 8 * SLICE, 0, 48, peer_core),
            (unit(0, y_far, 0), 48, SLICE, peer_up),
            (unit(0, y_far, 1), 54, SLICE, peer_down),
            (unit(0, y_up, 0), 60, 2 * SLICE, peer_up),
            (unit(0, y_down, 0), 72, 2 * SLICE, peer_down),
            (unit(0, y, 1 - z_lo), 84, SLICE, peer_z),
            (unit(0, y, z_lo), 90, SLICE, mirror),
        ),
        (
            ((1 - core) * 8 * SLICE, 0, 48, peer_core),
            (unit(1, y_far, z_lo), 48, half, peer_up),
            (unit(1, y_far, z_lo) + half, 51, half, peer_down),
            (unit(1, y_up, z_lo), 54, SLICE, peer_up),
            (unit(1, y_down, z_lo), 60, SLICE, peer_down),
            (unit(1, 0, 1 - z_lo), 66, 4 * SLICE, peer_z),
            (unit(1, y, z_lo), 90, SLICE, mirror),
        ),
    )

    def share_copy(role, proj, number):
        source, landing, count, peer = copies[proj][number]
        return pltpu.make_async_remote_copy(
            src_ref=W.at[role, proj, pl.ds(source, count)],
            dst_ref=WT.at[role, proj, pl.ds(landing, count)],
            send_sem=share_send.at[role, proj, number],
            recv_sem=share_recv.at[role, proj, number],
            device_id=peer,
            device_id_type=MESH,
        )

    def add(role, proj, place, *numbers):
        for number in numbers:
            share_copy(role, proj, number).wait_recv()

        def step(n, c):
            total = W[role, proj, place + n].astype(f32)
            for number in numbers:
                total = total + WT[role, proj, copies[proj][number][1] + n].astype(f32)
            W[role, proj, place + n] = total.astype(bf16)
            return c

        lax.fori_loop(0, copies[proj][numbers[0]][2], step, 0, unroll=3)

    def send(role, proj, *numbers):
        for number in numbers:
            share_copy(role, proj, number).start()

    def action(code):
        step, role = (code - 4 * chunks) // 2, (code - 4 * chunks) % 2
        owner = own == role

        def wait_ready(number):
            pl.semaphore_wait(ready_sem.at[role, number], 1)

        def send_mirror(proj):
            @pl.when(jnp.logical_not(owner))
            def _():
                if proj == 0:
                    wait_ready(4)
                send(role, proj, MIRROR)

        @pl.when(step == 0)
        def _():
            for number, peer in enumerate(peers[:4]):
                pl.semaphore_signal(ready_sem.at[role, number], inc=1, device_id=peer, device_id_type=MESH)

            @pl.when(owner)
            def _():
                pl.semaphore_signal(ready_sem.at[role, 4], inc=1, device_id=mirror, device_id_type=MESH)

            weight_gradient(role, 1)
            wait_ready(0)
            send(role, 1, CORE)
            weight_gradient(role, 0)
            send(role, 0, CORE)

        @pl.when(step == 1)
        def _():
            add(role, 1, mine, CORE)
            wait_ready(3)
            send(role, 1, Z)
            add(role, 0, mine, CORE)
            wait_ready(1)
            wait_ready(2)
            send(role, 0, FAR_UP, FAR_DOWN)

        @pl.when(step == 2)
        def _():
            add(role, 0, unit(0, y_up, 0), FAR_UP)
            send(role, 0, UP)
            add(role, 0, unit(0, y_down, 1), FAR_DOWN)
            send(role, 0, DOWN)

        @pl.when(step == 3)
        def _():
            add(role, 0, unit(0, y, 0), UP, DOWN)
            send(role, 0, Z)
            add(role, 1, unit(1, 0, z_lo), Z)
            send(role, 1, FAR_UP, FAR_DOWN)

        @pl.when(step == 4)
        def _():
            add(role, 1, unit(1, y_up, z_lo), FAR_UP)
            send(role, 1, UP)
            add(role, 1, unit(1, y_down, z_lo) + half, FAR_DOWN)
            send(role, 1, DOWN)
            add(role, 0, unit(0, y, z_lo), Z)
            send_mirror(0)

        @pl.when(step == 5)
        def _():
            add(role, 1, unit(1, y, z_lo), UP, DOWN)
            send_mirror(1)

        @pl.when(jnp.logical_and(step == 6, owner))
        def _():
            for proj in range(2):
                share_copy(role, proj, MIRROR).wait_recv()
                for n in range(SLICE):
                    there = WT[role, proj, 90 + n].astype(f32)
                    sums_out[proj, n] = W[role, proj, unit(proj, y, z_lo) + n].astype(f32) + there

    def turn(i, carry):
        code = jnp.int32(0)
        for t in range(len(sequences[0])):
            code = jnp.where(i == t, pick(stage, [o[t] for o in sequences]), code)

        @pl.when(i == jnp.where(stage < 2, chunks, 0))
        def _():
            transpose_weights()

        @pl.when(code < 4 * chunks)
        def _():
            item(code)

        @pl.when(code >= 4 * chunks)
        def _():
            action(code)

        return carry

    lax.fori_loop(0, len(sequences[0]), turn, 0)

    def drain(i, carry):
        op, chunk = i // chunks, i % chunks
        even = op % 2 == 0
        target = jnp.where(even, upper, lower)
        final = jnp.where(even, stage == STAGES - 1, stage == 0)

        @pl.when(jnp.logical_not(final))
        def _():
            link(op, chunk, target).wait_send()

        return carry

    lax.fori_loop(0, 4 * chunks, drain, 0)
    for role in range(2):
        for proj in range(2):
            for number in range(MIRROR):
                share_copy(role, proj, number).wait_send()

            @pl.when(own != role)
            def _(role=role, proj=proj):
                share_copy(role, proj, MIRROR).wait_send()


def adam_update(grad_sum, master, moment, variance, token_total):
    gradient = grad_sum / token_total
    moment_next = beta_first * moment + (1.0 - beta_first) * gradient
    variance_next = beta_second * variance + (1.0 - beta_second) * gradient * gradient
    corrected = moment_next / (1.0 - beta_first**update_count)
    spread = jnp.sqrt(variance_next / (1.0 - beta_second**update_count))
    step_direction = corrected / (spread + adam_eps)
    return (step_direction, master - learn_rate * (step_direction + decay_rate * master))


def shards(tokens, targets, weights, pattern, master, moment, variance):
    dp_size = lax.axis_size("dp")
    row_count = tokens.shape[1] * tokens.shape[2]
    chunks = row_count // ROWS

    index, keeps = tables(pattern[0])
    orders = make_orders(chunks, 2.6, 2.5, 4.5)
    smem = pl.BlockSpec(memory_space=pltpu.SMEM)
    anywhere = pl.BlockSpec(memory_space=pl.ANY)
    grads = pl.pallas_call(
        functools.partial(pipeline_kernel, chunks, make_sequences(chunks, orders)),
        out_shape=jax.ShapeDtypeStruct((2, SLICE, BS, BS), f32),
        in_specs=[smem, smem, anywhere, anywhere, anywhere],
        out_specs=pl.BlockSpec(memory_space=pltpu.VMEM),
        scratch_shapes=[
            pltpu.VMEM((2, 2, NNZ, BS, BS), bf16),
            pltpu.VMEM((2, 2, NNZ, BS, BS), bf16),
            pltpu.VMEM((4, DB, row_count, BS), bf16),
            pltpu.VMEM((4, DB, row_count, BS), bf16),
            pltpu.VMEM((2, DB, row_count, BS), bf16),
            pltpu.VMEM((2, DB, row_count, BS), bf16),
            pltpu.VMEM((2, FB, row_count, BS), bf16),
            pltpu.VMEM((2, FB, row_count, BS), bf16),
            pltpu.VMEM((DB, row_count, BS), bf16),
            pltpu.VMEM((NNZ + 1, ROWS, BS), f32),
            pltpu.SemaphoreType.DMA((2, 2)),
            pltpu.SemaphoreType.DMA((2, DB)),
            pltpu.SemaphoreType.DMA((4, chunks)),
            pltpu.SemaphoreType.DMA((4, chunks)),
            pltpu.SemaphoreType.DMA((2, 2, 7)),
            pltpu.SemaphoreType.DMA((2, 2, 7)),
            pltpu.SemaphoreType.REGULAR((2, 5)),
        ],
        compiler_params=pltpu.CompilerParams(
            collective_id=0, has_side_effects=True, vmem_limit_bytes=60 * 1024 * 1024
        ),
    )(index, keeps, tokens.reshape(2, row_count, D), targets.reshape(2, row_count, D), weights[0])

    token_total = 2 * row_count * dp_size
    step_direction, master_next = adam_update(
        grads.reshape(master.shape[1:]), master[0], moment[0], variance[0], token_total
    )
    return (step_direction[None], master_next[None])


def solution(mesh):
    return jax.shard_map(
        shards,
        mesh=mesh,
        in_specs=(
            P(None, None, "dp", None),
            P(None, None, "dp", None),
            P("section", None, None, None, None, None),
            P("section", None, None, None, None),
            P("section", None, None, "dp", None),
            P("section", None, None, "dp", None),
            P("section", None, None, "dp", None),
        ),
        out_specs=(P("section", None, None, "dp", None), P("section", None, None, "dp", None)),
        check_vma=False,
    )
```

```python
import functools

import jax
import jax.numpy as jnp
from jax import lax
from jax.experimental import pallas as pl
from jax.experimental.pallas import tpu as pltpu
from jax.sharding import PartitionSpec as P

D = 2048
FF = 8192
BS = 128
NNZ = 96
DB = D // BS
FB = FF // BS
STAGES = 4
ROWS = 32
STEPS = 7
SLICE = 6

norm_eps = 1e-06
gelu_coef = 0.7978845608028654
beta_first = 0.9
beta_second = 0.95
adam_eps = 1e-08
learn_rate = 0.001
decay_rate = 0.1
update_count = 10

MESH = pl.DeviceIdType.MESH
f32 = jnp.float32
bf16 = jnp.bfloat16

UPF_ROW, UPF_PERM, UP_LAST = 0, 96, 192
DNF_ROW, DNF_PERM, DN_LAST = 256, 352, 448
VB_COL, VB_LAST = 464, 560
UB_COL, UB_LAST = 624, 720
U_ROW, V_ROW = 736, 832
TABLE = 928
K_UPF, K_DNF, K_VB, K_UB, KEEPS = 0, 96, 192, 288, 384


def make_orders(chunks, cost_forward, cost_backward, hop):
    arrival = {(0, 0, c): 0.0 for c in range(chunks)}
    free = [0.0] * STAGES
    orders = [[] for _ in range(STAGES)]
    for _ in range(4 * STAGES * chunks):
        start, later, chunk, stage = min(
            (max(t, free[s]), -op, c, s) for (s, op, c), t in arrival.items()
        )
        op = -later
        del arrival[(stage, op, chunk)]
        end = start + (cost_forward if op < 2 else cost_backward)
        free[stage] = end
        orders[stage].append(op * chunks + chunk)
        following = stage + (1 if op % 2 == 0 else -1)
        if 0 <= following < STAGES:
            arrival[(following, op, chunk)] = end + hop
        elif op < 3:
            arrival[(stage, op + 1, chunk)] = end
    return orders


def make_sequences(chunks, orders):
    items = 4 * chunks
    sequences = []
    for order in orders:
        turn = order.index(2 * chunks + chunks - 1)
        code = lambda step, role: items + 2 * step + role
        first = [(turn, 0)] + [(turn + gap, step) for step, gap in ((1, 2), (2, 3), (3, 6))]
        placed = {}
        for at, step in first:
            if at < items - 1 and turn < items - 2:
                placed.setdefault(at, []).append(code(step, 1))
        sequence = []
        for n, item in enumerate(order):
            sequence.append(item)
            sequence.extend(placed.get(n, []))
        done = sum(len(v) for v in placed.values())
        early = [code(step, 1) for step in range(done, STEPS)]
        late = [code(step, 0) for step in range(STEPS)]
        if done == 0:
            sequence.extend([early.pop(0), early.pop(0), late.pop(0)])
        else:
            sequence.extend([late.pop(0), late.pop(0)])
        while early or late:
            if early:
                sequence.append(early.pop(0))
            if late:
                sequence.append(late.pop(0))
        sequences.append(sequence)
    return sequences


def tables(pattern):
    rows, cols = pattern[..., 0], pattern[..., 1]
    key = cols * 64 + rows
    rank = jnp.sum((key[..., None, :] < key[..., :, None]).astype(jnp.int32), axis=-1)
    slots = jnp.arange(NNZ, dtype=jnp.int32)
    hit = (rank[..., None, :] == slots[:, None]).astype(jnp.int32)
    perm = jnp.sum(hit * slots, axis=-1)
    sorted_rows = jnp.sum(hit * rows[..., None, :], axis=-1)
    sorted_cols = jnp.sum(hit * cols[..., None, :], axis=-1)

    def last(values, count):
        bins = jnp.arange(count, dtype=jnp.int32)[:, None]
        through = jnp.sum((values[..., None, :] <= bins).astype(jnp.int32), axis=-1)
        here = jnp.sum((values[..., None, :] == bins).astype(jnp.int32), axis=-1)
        return jnp.where(here > 0, through - 1, NNZ)

    def keep(values):
        same = (values[..., 1:] == values[..., :-1]).astype(f32)
        return jnp.concatenate([jnp.zeros_like(same[..., :1]), same], axis=-1)

    index = jnp.concatenate(
        [
            sorted_rows[:, 0],
            perm[:, 0],
            last(cols[:, 0], FB),
            sorted_rows[:, 1],
            perm[:, 1],
            last(cols[:, 1], DB),
            cols[:, 1],
            last(rows[:, 1], FB),
            cols[:, 0],
            last(rows[:, 0], DB),
            rows[:, 0],
            rows[:, 1],
        ],
        axis=-1,
    )
    keeps = jnp.concatenate(
        [keep(sorted_cols[:, 0]), keep(sorted_cols[:, 1]), keep(rows[:, 1]), keep(rows[:, 0])],
        axis=-1,
    )
    return index.reshape(-1), keeps.reshape(-1)


def pick(stage, values):
    out = jnp.int32(values[0])
    for s in range(1, STAGES):
        out = jnp.where(stage == s, jnp.int32(values[s]), out)
    return out


def pipeline_kernel(
    chunks,
    sequences,
    tab,
    keeps,
    tok,
    tgt,
    wts,
    sums_out,
    W,
    WT,
    ACT,
    OUT,
    COT,
    NORM,
    H,
    S,
    TG,
    PS,
    w_sem,
    t_sem,
    send_sem,
    recv_sem,
    share_send,
    share_recv,
    ready_sem,
):
    R = ROWS
    total_rows = chunks * R
    section = lax.axis_index("section")
    dp = lax.axis_index("dp")
    z_hi = section % 2
    stage = jnp.where(section < 4, section, 7 - section)
    own = jnp.where(section < 4, 0, 1)

    core, z_lo, y = dp % 2, (dp // 2) % 2, dp // 4
    def section_of(s):
        return jnp.where(s % 2 == z_hi, s, 7 - s)

    upper = section_of(jnp.minimum(stage + 1, STAGES - 1))
    lower = section_of(jnp.maximum(stage - 1, 0))
    y_up, y_down, y_far = (y + 1) % 4, (y + 3) % 4, (y + 2) % 4
    peer_core = (section, dp + 1 - 2 * core)
    peer_up = (section, y_up * 4 + z_lo * 2 + core)
    peer_down = (section, y_down * 4 + z_lo * 2 + core)
    peer_z = (section, dp + 2 - 4 * z_lo)
    mirror = (7 - section, dp)
    peers = (peer_core, peer_up, peer_down, peer_z, mirror)

    barrier = pltpu.get_barrier_semaphore()

    @pl.when(stage < STAGES - 1)
    def _():
        pl.semaphore_signal(barrier, inc=1, device_id=(upper, dp), device_id_type=MESH)

    @pl.when(stage > 0)
    def _():
        pl.semaphore_signal(barrier, inc=1, device_id=(lower, dp), device_id_type=MESH)

    for peer in peers:
        pl.semaphore_signal(barrier, inc=1, device_id=peer, device_id_type=MESH)

    def weight_copy(layer, proj):
        copy = own if layer == 0 else 1 - own
        return pltpu.make_async_copy(wts.at[copy, proj], W.at[layer, proj], w_sem.at[layer, proj])

    for layer in range(2):
        for proj in range(2):
            weight_copy(layer, proj).start()

    def row_copies():
        for b in range(DB):
            columns = pl.ds(b * BS, BS)
            yield pltpu.make_async_copy(tok.at[z_hi, :, columns], ACT.at[0, b], t_sem.at[0, b])
        for b in range(DB):
            columns = pl.ds(b * BS, BS)
            yield pltpu.make_async_copy(tgt.at[z_hi, :, columns], TG.at[b], t_sem.at[1, b])

    @pl.when(stage == 0)
    def _():
        for copy in row_copies():
            copy.start()

    PS[NNZ] = jnp.zeros((R, BS), f32)

    pl.semaphore_wait(barrier, jnp.where((stage == 0) | (stage == STAGES - 1), 6, 7))

    for layer in range(2):
        for proj in range(2):
            weight_copy(layer, proj).wait()

    @pl.when(stage == 0)
    def _():
        for copy in row_copies():
            copy.wait()

    def link(op, chunk, target):
        rows = pl.ds(pl.multiple_of(chunk * R, R), R)
        return pltpu.make_async_remote_copy(
            src_ref=OUT.at[op, :, rows, :],
            dst_ref=ACT.at[op, :, rows, :],
            send_sem=send_sem.at[op, chunk],
            recv_sem=recv_sem.at[op, chunk],
            device_id=(target, dp),
            device_id_type=MESH,
        )

    def chain(keep_base, lhs, block, group=16, then=None):
        acc = jnp.zeros((R, BS), f32)
        done = 0
        for first in range(0, NNZ, group):
            slots = range(first, first + group)
            products = [jnp.dot(lhs(k), block(k), preferred_element_type=f32) for k in slots]
            stores = []
            if then is not None:
                ended = max(0, first - (NNZ - FB))
                stores = [then(j) for j in range(done, ended)]
                done = ended
            sums = []
            for u in range(group):
                acc = acc * keeps[keep_base + first + u] + products[u]
                sums.append(acc)
            for u in range(group):
                PS[first + u] = sums[u]
            for store in stores:
                store()
        if then is not None:
            for store in [then(j) for j in range(done, FB)]:
                store()

    def transpose_weights():
        def step(outer, c):
            for layer in range(2):
                for proj in range(2):
                    turned = [W[layer, proj, outer * 8 + u].T for u in range(8)]
                    for u in range(8):
                        WT[layer, proj, outer * 8 + u] = turned[u]
            return c

        lax.fori_loop(0, NNZ // 8, step, 0)

    def item(code):
        op, chunk = code // chunks, code % chunks
        layer = jnp.where((op == 1) | (op == 2), 1, 0)
        copy = jnp.where(layer == 0, own, 1 - own)
        base = copy * TABLE
        keep_base = copy * KEEPS
        rows = pl.ds(pl.multiple_of(chunk * R, R), R)
        even = op % 2 == 0
        source = jnp.where(even, lower, upper)
        target = jnp.where(even, upper, lower)
        first = jnp.where(even, stage == 0, stage == STAGES - 1)
        final = jnp.where(even, stage == STAGES - 1, stage == 0)

        @pl.when(jnp.logical_not(first))
        def _():
            link(op, chunk, source).wait_recv()

        def factor_of(act_op):
            def square(b, acc):
                v = ACT[act_op, b, rows, :].astype(f32)
                return acc + v * v

            total = lax.fori_loop(0, DB, square, jnp.zeros((R, BS), f32), unroll=True)
            return lax.rsqrt(jnp.sum(total, axis=-1, keepdims=True) * (1.0 / D) + norm_eps)

        @pl.when(op < 2)
        def _():
            factor = factor_of(op)

            def normalize(b, c):
                v = ACT[op, b, rows, :].astype(f32)
                NORM[layer, b, rows, :] = (v * factor).astype(bf16)
                return c

            lax.fori_loop(0, DB, normalize, 0, unroll=True)
            def activate(j):
                a = PS[tab[base + UP_LAST + j]]
                sq = a * a
                th = jnp.tanh(a * (gelu_coef + (gelu_coef * 0.044715) * sq))
                half = 0.5 + 0.5 * th
                slope = half + (0.5 * a) * (1.0 - th * th) * (
                    gelu_coef + (gelu_coef * 3.0 * 0.044715) * sq
                )
                hidden = (a * half).astype(bf16)
                slope = slope.astype(bf16)

                def store():
                    H[layer, j, rows, :] = hidden
                    S[layer, j, rows, :] = slope

                return store

            chain(
                keep_base + K_UPF,
                lambda k: NORM[layer, tab[base + UPF_ROW + k], rows, :],
                lambda k: W[layer, 0, tab[base + UPF_PERM + k]],
                group=8,
                then=activate,
            )
            chain(
                keep_base + K_DNF,
                lambda k: H[layer, tab[base + DNF_ROW + k], rows, :],
                lambda k: W[layer, 1, tab[base + DNF_PERM + k]],
            )

            def mixed(b):
                v = ACT[op, b, rows, :].astype(f32)
                return (v + PS[tab[base + DN_LAST + b]]).astype(bf16)

            @pl.when(jnp.logical_not(final))
            def _():
                def put(b, c):
                    OUT[op, b, rows, :] = mixed(b)
                    return c

                lax.fori_loop(0, DB, put, 0, unroll=True)

            @pl.when(jnp.logical_and(final, op == 0))
            def _():
                def put(b, c):
                    ACT[1, b, rows, :] = mixed(b)
                    return c

                lax.fori_loop(0, DB, put, 0, unroll=True)

            @pl.when(jnp.logical_and(final, op == 1))
            def _():
                def put(b, c):
                    residue = mixed(b).astype(f32) - TG[b, rows, :].astype(f32)
                    ACT[2, b, rows, :] = residue.astype(bf16)
                    return c

                lax.fori_loop(0, DB, put, 0, unroll=True)

        @pl.when(op >= 2)
        def _():
            inputs = 3 - op
            for b in range(DB):
                COT[layer, b, rows, :] = ACT[op, b, rows, :]
            def slope_times(j):
                g = PS[tab[base + VB_LAST + j]]
                result = (g * S[layer, j, rows, :].astype(f32)).astype(bf16)

                def store():
                    S[layer, j, rows, :] = result

                return store

            chain(
                keep_base + K_VB,
                lambda k: COT[layer, tab[base + VB_COL + k], rows, :],
                lambda k: WT[layer, 1, k],
                then=slope_times,
            )

            @pl.when(jnp.logical_not(jnp.logical_and(final, op == 3)))
            def _():
                chain(
                    keep_base + K_UB,
                    lambda k: S[layer, tab[base + UB_COL + k], rows, :],
                    lambda k: WT[layer, 0, k],
                )
                factor = factor_of(inputs)

                def couple(b, acc):
                    v = ACT[inputs, b, rows, :].astype(f32)
                    return acc + v * PS[tab[base + UB_LAST + b]]

                coupling = lax.fori_loop(0, DB, couple, jnp.zeros((R, BS), f32), unroll=True)
                coupling = jnp.sum(coupling, axis=-1, keepdims=True) * (1.0 / D)
                pull = factor * factor * factor * coupling

                def downstream(b):
                    v = ACT[inputs, b, rows, :].astype(f32)
                    g = PS[tab[base + UB_LAST + b]]
                    return (ACT[op, b, rows, :].astype(f32) + factor * g - v * pull).astype(bf16)

                @pl.when(jnp.logical_not(final))
                def _():
                    def put(b, c):
                        OUT[op, b, rows, :] = downstream(b)
                        return c

                    lax.fori_loop(0, DB, put, 0, unroll=True)

                @pl.when(final)
                def _():
                    def put(b, c):
                        ACT[3, b, rows, :] = downstream(b)
                        return c

                    lax.fori_loop(0, DB, put, 0, unroll=True)

        @pl.when(jnp.logical_not(final))
        def _():
            link(op, chunk, target).start()

    def pair(lhs, rhs):
        return lax.dot_general(lhs, rhs, (((0,), (0,)), ((), ())), preferred_element_type=f32)

    def weight_gradient(role, proj):
        base = jnp.where(role == 0, own, 1 - own) * TABLE

        def blocks(outer, c):
            parts = []
            for u in range(16):
                k = outer * 16 + u
                if proj == 0:
                    lhs = NORM[role, tab[base + U_ROW + k]]
                    rhs = S[role, tab[base + UB_COL + k]]
                else:
                    lhs = H[role, tab[base + V_ROW + k]]
                    rhs = COT[role, tab[base + VB_COL + k]]
                parts.append(pair(lhs, rhs))
            for v in range(8):
                for d in range(16):
                    both = jnp.concatenate(
                        [p[8 * d : 8 * d + 8] for p in parts[2 * v : 2 * v + 2]], axis=0
                    )
                    of_core, of_y, of_z = d % 2, d // 4, (d // 2) % 2
                    place = of_core * 8 + (of_y * 2 + of_z if proj == 0 else of_z * 4 + of_y)
                    W[role, proj, place * SLICE + outer, 16 * v : 16 * v + 16, :] = both.astype(bf16)
            return c

        lax.fori_loop(0, SLICE, blocks, 0)

    mine = core * 8 * SLICE

    def unit(proj, of_y, of_z):
        return mine + (of_y * 2 + of_z if proj == 0 else of_z * 4 + of_y) * SLICE

    CORE, FAR_UP, FAR_DOWN, UP, DOWN, Z, MIRROR = range(7)
    half = SLICE // 2
    copies = (
        (
            ((1 - core) * 8 * SLICE, 0, 48, peer_core),
            (unit(0, y_far, 0), 48, SLICE, peer_up),
            (unit(0, y_far, 1), 54, SLICE, peer_down),
            (unit(0, y_up, 0), 60, 2 * SLICE, peer_up),
            (unit(0, y_down, 0), 72, 2 * SLICE, peer_down),
            (unit(0, y, 1 - z_lo), 84, SLICE, peer_z),
            (unit(0, y, z_lo), 90, SLICE, mirror),
        ),
        (
            ((1 - core) * 8 * SLICE, 0, 48, peer_core),
            (unit(1, y_far, z_lo), 48, half, peer_up),
            (unit(1, y_far, z_lo) + half, 51, half, peer_down),
            (unit(1, y_up, z_lo), 54, SLICE, peer_up),
            (unit(1, y_down, z_lo), 60, SLICE, peer_down),
            (unit(1, 0, 1 - z_lo), 66, 4 * SLICE, peer_z),
            (unit(1, y, z_lo), 90, SLICE, mirror),
        ),
    )

    def share_copy(role, proj, number):
        source, landing, count, peer = copies[proj][number]
        return pltpu.make_async_remote_copy(
            src_ref=W.at[role, proj, pl.ds(source, count)],
            dst_ref=WT.at[role, proj, pl.ds(landing, count)],
            send_sem=share_send.at[role, proj, number],
            recv_sem=share_recv.at[role, proj, number],
            device_id=peer,
            device_id_type=MESH,
        )

    def add(role, proj, place, *numbers):
        for number in numbers:
            share_copy(role, proj, number).wait_recv()

        def step(n, c):
            total = W[role, proj, place + n].astype(f32)
            for number in numbers:
                total = total + WT[role, proj, copies[proj][number][1] + n].astype(f32)
            W[role, proj, place + n] = total.astype(bf16)
            return c

        lax.fori_loop(0, copies[proj][numbers[0]][2], step, 0, unroll=3)

    def send(role, proj, *numbers):
        for number in numbers:
            share_copy(role, proj, number).start()

    def action(code):
        step, role = (code - 4 * chunks) // 2, (code - 4 * chunks) % 2
        owner = own == role

        def wait_ready(number):
            pl.semaphore_wait(ready_sem.at[role, number], 1)

        def send_mirror(proj):
            @pl.when(jnp.logical_not(owner))
            def _():
                if proj == 0:
                    wait_ready(4)
                send(role, proj, MIRROR)

        @pl.when(step == 0)
        def _():
            for number, peer in enumerate(peers[:4]):
                pl.semaphore_signal(ready_sem.at[role, number], inc=1, device_id=peer, device_id_type=MESH)

            @pl.when(owner)
            def _():
                pl.semaphore_signal(ready_sem.at[role, 4], inc=1, device_id=mirror, device_id_type=MESH)

            weight_gradient(role, 1)
            wait_ready(0)
            send(role, 1, CORE)
            weight_gradient(role, 0)
            send(role, 0, CORE)

        @pl.when(step == 1)
        def _():
            add(role, 1, mine, CORE)
            wait_ready(3)
            send(role, 1, Z)
            add(role, 0, mine, CORE)
            wait_ready(1)
            wait_ready(2)
            send(role, 0, FAR_UP, FAR_DOWN)

        @pl.when(step == 2)
        def _():
            add(role, 0, unit(0, y_up, 0), FAR_UP)
            send(role, 0, UP)
            add(role, 0, unit(0, y_down, 1), FAR_DOWN)
            send(role, 0, DOWN)

        @pl.when(step == 3)
        def _():
            add(role, 0, unit(0, y, 0), UP, DOWN)
            send(role, 0, Z)
            add(role, 1, unit(1, 0, z_lo), Z)
            send(role, 1, FAR_UP, FAR_DOWN)

        @pl.when(step == 4)
        def _():
            add(role, 1, unit(1, y_up, z_lo), FAR_UP)
            send(role, 1, UP)
            add(role, 1, unit(1, y_down, z_lo) + half, FAR_DOWN)
            send(role, 1, DOWN)
            add(role, 0, unit(0, y, z_lo), Z)
            send_mirror(0)

        @pl.when(step == 5)
        def _():
            add(role, 1, unit(1, y, z_lo), UP, DOWN)
            send_mirror(1)

        @pl.when(jnp.logical_and(step == 6, owner))
        def _():
            for proj in range(2):
                share_copy(role, proj, MIRROR).wait_recv()
                for n in range(SLICE):
                    there = WT[role, proj, 90 + n].astype(f32)
                    sums_out[proj, n] = W[role, proj, unit(proj, y, z_lo) + n].astype(f32) + there

    def turn(i, carry):
        code = jnp.int32(0)
        for t in range(len(sequences[0])):
            code = jnp.where(i == t, pick(stage, [o[t] for o in sequences]), code)

        @pl.when(i == jnp.where(stage < 2, chunks, 0))
        def _():
            transpose_weights()

        @pl.when(code < 4 * chunks)
        def _():
            item(code)

        @pl.when(code >= 4 * chunks)
        def _():
            action(code)

        return carry

    lax.fori_loop(0, len(sequences[0]), turn, 0)

    def drain(i, carry):
        op, chunk = i // chunks, i % chunks
        even = op % 2 == 0
        target = jnp.where(even, upper, lower)
        final = jnp.where(even, stage == STAGES - 1, stage == 0)

        @pl.when(jnp.logical_not(final))
        def _():
            link(op, chunk, target).wait_send()

        return carry

    lax.fori_loop(0, 4 * chunks, drain, 0)
    for role in range(2):
        for proj in range(2):
            for number in range(MIRROR):
                share_copy(role, proj, number).wait_send()

            @pl.when(own != role)
            def _(role=role, proj=proj):
                share_copy(role, proj, MIRROR).wait_send()


def adam_update(grad_sum, master, moment, variance, token_total):
    gradient = grad_sum / token_total
    moment_next = beta_first * moment + (1.0 - beta_first) * gradient
    variance_next = beta_second * variance + (1.0 - beta_second) * gradient * gradient
    corrected = moment_next / (1.0 - beta_first**update_count)
    spread = jnp.sqrt(variance_next / (1.0 - beta_second**update_count))
    step_direction = corrected / (spread + adam_eps)
    return (step_direction, master - learn_rate * (step_direction + decay_rate * master))


def shards(tokens, targets, weights, pattern, master, moment, variance):
    dp_size = lax.axis_size("dp")
    row_count = tokens.shape[1] * tokens.shape[2]
    chunks = row_count // ROWS

    index, keeps = tables(pattern[0])
    orders = make_orders(chunks, 2.6, 2.5, 4.5)
    smem = pl.BlockSpec(memory_space=pltpu.SMEM)
    anywhere = pl.BlockSpec(memory_space=pl.ANY)
    grads = pl.pallas_call(
        functools.partial(pipeline_kernel, chunks, make_sequences(chunks, orders)),
        out_shape=jax.ShapeDtypeStruct((2, SLICE, BS, BS), f32),
        in_specs=[smem, smem, anywhere, anywhere, anywhere],
        out_specs=pl.BlockSpec(memory_space=pltpu.VMEM),
        scratch_shapes=[
            pltpu.VMEM((2, 2, NNZ, BS, BS), bf16),
            pltpu.VMEM((2, 2, NNZ, BS, BS), bf16),
            pltpu.VMEM((4, DB, row_count, BS), bf16),
            pltpu.VMEM((4, DB, row_count, BS), bf16),
            pltpu.VMEM((2, DB, row_count, BS), bf16),
            pltpu.VMEM((2, DB, row_count, BS), bf16),
            pltpu.VMEM((2, FB, row_count, BS), bf16),
            pltpu.VMEM((2, FB, row_count, BS), bf16),
            pltpu.VMEM((DB, row_count, BS), bf16),
            pltpu.VMEM((NNZ + 1, ROWS, BS), f32),
            pltpu.SemaphoreType.DMA((2, 2)),
            pltpu.SemaphoreType.DMA((2, DB)),
            pltpu.SemaphoreType.DMA((4, chunks)),
            pltpu.SemaphoreType.DMA((4, chunks)),
            pltpu.SemaphoreType.DMA((2, 2, 7)),
            pltpu.SemaphoreType.DMA((2, 2, 7)),
            pltpu.SemaphoreType.REGULAR((2, 5)),
        ],
        compiler_params=pltpu.CompilerParams(
            collective_id=0, has_side_effects=True, vmem_limit_bytes=60 * 1024 * 1024
        ),
    )(index, keeps, tokens.reshape(2, row_count, D), targets.reshape(2, row_count, D), weights[0])

    token_total = 2 * row_count * dp_size
    step_direction, master_next = adam_update(
        grads.reshape(master.shape[1:]), master[0], moment[0], variance[0], token_total
    )
    return (step_direction[None], master_next[None])


def solution(mesh):
    return jax.shard_map(
        shards,
        mesh=mesh,
        in_specs=(
            P(None, None, "dp", None),
            P(None, None, "dp", None),
            P("section", None, None, None, None, None),
            P("section", None, None, None, None),
            P("section", None, None, "dp", None),
            P("section", None, None, "dp", None),
            P("section", None, None, "dp", None),
        ),
        out_specs=(P("section", None, None, "dp", None), P("section", None, None, "dp", None)),
        check_vma=False,
    )
```

```python
import functools

import jax
import jax.numpy as jnp
from jax import lax
from jax.experimental import pallas as pl
from jax.experimental.pallas import tpu as pltpu
from jax.sharding import PartitionSpec as P

D = 2048
FF = 8192
BS = 128
NNZ = 96
DB = D // BS
FB = FF // BS
STAGES = 4
ROWS = 32
STEPS = 7
SLICE = 6

norm_eps = 1e-06
gelu_coef = 0.7978845608028654
beta_first = 0.9
beta_second = 0.95
adam_eps = 1e-08
learn_rate = 0.001
decay_rate = 0.1
update_count = 10

MESH = pl.DeviceIdType.MESH
f32 = jnp.float32
bf16 = jnp.bfloat16

UPF_ROW, UPF_PERM, UP_LAST = 0, 96, 192
DNF_ROW, DNF_PERM, DN_LAST = 256, 352, 448
VB_COL, VB_LAST = 464, 560
UB_COL, UB_LAST = 624, 720
U_ROW, V_ROW = 736, 832
TABLE = 928
K_UPF, K_DNF, K_VB, K_UB, KEEPS = 0, 96, 192, 288, 384


def make_orders(chunks, cost_forward, cost_backward, hop):
    arrival = {(0, 0, c): 0.0 for c in range(chunks)}
    free = [0.0] * STAGES
    orders = [[] for _ in range(STAGES)]
    for _ in range(4 * STAGES * chunks):
        start, later, chunk, stage = min(
            (max(t, free[s]), -op, c, s) for (s, op, c), t in arrival.items()
        )
        op = -later
        del arrival[(stage, op, chunk)]
        end = start + (cost_forward if op < 2 else cost_backward)
        free[stage] = end
        orders[stage].append(op * chunks + chunk)
        following = stage + (1 if op % 2 == 0 else -1)
        if 0 <= following < STAGES:
            arrival[(following, op, chunk)] = end + hop
        elif op < 3:
            arrival[(stage, op + 1, chunk)] = end
    return orders


def make_sequences(chunks, orders):
    items = 4 * chunks
    sequences = []
    for order in orders:
        turn = order.index(2 * chunks + chunks - 1)
        code = lambda step, role: items + 2 * step + role
        first = [(turn, 0)] + [(turn + gap, step) for step, gap in ((1, 2), (2, 3), (3, 6))]
        placed = {}
        for at, step in first:
            if at < items - 1 and turn < items - 2:
                placed.setdefault(at, []).append(code(step, 1))
        sequence = []
        for n, item in enumerate(order):
            sequence.append(item)
            sequence.extend(placed.get(n, []))
        done = sum(len(v) for v in placed.values())
        early = [code(step, 1) for step in range(done, STEPS)]
        late = [code(step, 0) for step in range(STEPS)]
        if done == 0:
            sequence.append(early.pop(0))
        sequence.append(late.pop(0))
        while early or late:
            if early:
                sequence.append(early.pop(0))
            if late:
                sequence.append(late.pop(0))
        sequences.append(sequence)
    return sequences


def tables(pattern):
    rows, cols = pattern[..., 0], pattern[..., 1]
    key = cols * 64 + rows
    rank = jnp.sum((key[..., None, :] < key[..., :, None]).astype(jnp.int32), axis=-1)
    slots = jnp.arange(NNZ, dtype=jnp.int32)
    hit = (rank[..., None, :] == slots[:, None]).astype(jnp.int32)
    perm = jnp.sum(hit * slots, axis=-1)
    sorted_rows = jnp.sum(hit * rows[..., None, :], axis=-1)
    sorted_cols = jnp.sum(hit * cols[..., None, :], axis=-1)

    def last(values, count):
        bins = jnp.arange(count, dtype=jnp.int32)[:, None]
        through = jnp.sum((values[..., None, :] <= bins).astype(jnp.int32), axis=-1)
        here = jnp.sum((values[..., None, :] == bins).astype(jnp.int32), axis=-1)
        return jnp.where(here > 0, through - 1, NNZ)

    def keep(values):
        same = (values[..., 1:] == values[..., :-1]).astype(f32)
        return jnp.concatenate([jnp.zeros_like(same[..., :1]), same], axis=-1)

    index = jnp.concatenate(
        [
            sorted_rows[:, 0],
            perm[:, 0],
            last(cols[:, 0], FB),
            sorted_rows[:, 1],
            perm[:, 1],
            last(cols[:, 1], DB),
            cols[:, 1],
            last(rows[:, 1], FB),
            cols[:, 0],
            last(rows[:, 0], DB),
            rows[:, 0],
            rows[:, 1],
        ],
        axis=-1,
    )
    keeps = jnp.concatenate(
        [keep(sorted_cols[:, 0]), keep(sorted_cols[:, 1]), keep(rows[:, 1]), keep(rows[:, 0])],
        axis=-1,
    )
    return index.reshape(-1), keeps.reshape(-1)


def pick(stage, values):
    out = jnp.int32(values[0])
    for s in range(1, STAGES):
        out = jnp.where(stage == s, jnp.int32(values[s]), out)
    return out


def pipeline_kernel(
    chunks,
    sequences,
    tab,
    keeps,
    tok,
    tgt,
    wts,
    sums_out,
    W,
    WT,
    ACT,
    OUT,
    COT,
    NORM,
    H,
    S,
    TG,
    PS,
    w_sem,
    t_sem,
    send_sem,
    recv_sem,
    share_send,
    share_recv,
    ready_sem,
):
    R = ROWS
    total_rows = chunks * R
    section = lax.axis_index("section")
    dp = lax.axis_index("dp")
    z_hi = section % 2
    stage = jnp.where(section < 4, section, 7 - section)
    own = jnp.where(section < 4, 0, 1)

    core, z_lo, y = dp % 2, (dp // 2) % 2, dp // 4
    def section_of(s):
        return jnp.where(s % 2 == z_hi, s, 7 - s)

    upper = section_of(jnp.minimum(stage + 1, STAGES - 1))
    lower = section_of(jnp.maximum(stage - 1, 0))
    y_up, y_down, y_far = (y + 1) % 4, (y + 3) % 4, (y + 2) % 4
    peer_core = (section, dp + 1 - 2 * core)
    peer_up = (section, y_up * 4 + z_lo * 2 + core)
    peer_down = (section, y_down * 4 + z_lo * 2 + core)
    peer_z = (section, dp + 2 - 4 * z_lo)
    mirror = (7 - section, dp)
    peers = (peer_core, peer_up, peer_down, peer_z, mirror)

    barrier = pltpu.get_barrier_semaphore()

    @pl.when(stage < STAGES - 1)
    def _():
        pl.semaphore_signal(barrier, inc=1, device_id=(upper, dp), device_id_type=MESH)

    @pl.when(stage > 0)
    def _():
        pl.semaphore_signal(barrier, inc=1, device_id=(lower, dp), device_id_type=MESH)

    for peer in peers:
        pl.semaphore_signal(barrier, inc=1, device_id=peer, device_id_type=MESH)

    def weight_copy(layer, proj):
        copy = own if layer == 0 else 1 - own
        return pltpu.make_async_copy(wts.at[copy, proj], W.at[layer, proj], w_sem.at[layer, proj])

    for layer in range(2):
        for proj in range(2):
            weight_copy(layer, proj).start()

    def row_copies():
        for b in range(DB):
            columns = pl.ds(b * BS, BS)
            yield pltpu.make_async_copy(tok.at[z_hi, :, columns], ACT.at[0, b], t_sem.at[0, b])
        for b in range(DB):
            columns = pl.ds(b * BS, BS)
            yield pltpu.make_async_copy(tgt.at[z_hi, :, columns], TG.at[b], t_sem.at[1, b])

    @pl.when(stage == 0)
    def _():
        for copy in row_copies():
            copy.start()

    PS[NNZ] = jnp.zeros((R, BS), f32)

    pl.semaphore_wait(barrier, jnp.where((stage == 0) | (stage == STAGES - 1), 6, 7))

    for layer in range(2):
        for proj in range(2):
            weight_copy(layer, proj).wait()

    @pl.when(stage == 0)
    def _():
        for copy in row_copies():
            copy.wait()

    def link(op, chunk, target):
        rows = pl.ds(pl.multiple_of(chunk * R, R), R)
        return pltpu.make_async_remote_copy(
            src_ref=OUT.at[op, :, rows, :],
            dst_ref=ACT.at[op, :, rows, :],
            send_sem=send_sem.at[op, chunk],
            recv_sem=recv_sem.at[op, chunk],
            device_id=(target, dp),
            device_id_type=MESH,
        )

    def chain(keep_base, lhs, block, group=16, then=None):
        acc = jnp.zeros((R, BS), f32)
        done = 0
        for first in range(0, NNZ, group):
            slots = range(first, first + group)
            products = [jnp.dot(lhs(k), block(k), preferred_element_type=f32) for k in slots]
            stores = []
            if then is not None:
                ended = max(0, first - (NNZ - FB))
                stores = [then(j) for j in range(done, ended)]
                done = ended
            sums = []
            for u in range(group):
                acc = acc * keeps[keep_base + first + u] + products[u]
                sums.append(acc)
            for u in range(group):
                PS[first + u] = sums[u]
            for store in stores:
                store()
        if then is not None:
            for store in [then(j) for j in range(done, FB)]:
                store()

    def transpose_weights():
        def step(outer, c):
            for layer in range(2):
                for proj in range(2):
                    turned = [W[layer, proj, outer * 8 + u].T for u in range(8)]
                    for u in range(8):
                        WT[layer, proj, outer * 8 + u] = turned[u]
            return c

        lax.fori_loop(0, NNZ // 8, step, 0)

    def item(code):
        op, chunk = code // chunks, code % chunks
        layer = jnp.where((op == 1) | (op == 2), 1, 0)
        copy = jnp.where(layer == 0, own, 1 - own)
        base = copy * TABLE
        keep_base = copy * KEEPS
        rows = pl.ds(pl.multiple_of(chunk * R, R), R)
        even = op % 2 == 0
        source = jnp.where(even, lower, upper)
        target = jnp.where(even, upper, lower)
        first = jnp.where(even, stage == 0, stage == STAGES - 1)
        final = jnp.where(even, stage == STAGES - 1, stage == 0)

        @pl.when(jnp.logical_not(first))
        def _():
            link(op, chunk, source).wait_recv()

        def factor_of(act_op):
            def square(b, acc):
                v = ACT[act_op, b, rows, :].astype(f32)
                return acc + v * v

            total = lax.fori_loop(0, DB, square, jnp.zeros((R, BS), f32), unroll=True)
            return lax.rsqrt(jnp.sum(total, axis=-1, keepdims=True) * (1.0 / D) + norm_eps)

        @pl.when(op < 2)
        def _():
            factor = factor_of(op)

            def normalize(b, c):
                v = ACT[op, b, rows, :].astype(f32)
                NORM[layer, b, rows, :] = (v * factor).astype(bf16)
                return c

            lax.fori_loop(0, DB, normalize, 0, unroll=True)
            def activate(j):
                a = PS[tab[base + UP_LAST + j]]
                sq = a * a
                th = jnp.tanh(a * (gelu_coef + (gelu_coef * 0.044715) * sq))
                half = 0.5 + 0.5 * th
                slope = half + (0.5 * a) * (1.0 - th * th) * (
                    gelu_coef + (gelu_coef * 3.0 * 0.044715) * sq
                )
                hidden = (a * half).astype(bf16)
                slope = slope.astype(bf16)

                def store():
                    H[layer, j, rows, :] = hidden
                    S[layer, j, rows, :] = slope

                return store

            chain(
                keep_base + K_UPF,
                lambda k: NORM[layer, tab[base + UPF_ROW + k], rows, :],
                lambda k: W[layer, 0, tab[base + UPF_PERM + k]],
                group=8,
                then=activate,
            )
            chain(
                keep_base + K_DNF,
                lambda k: H[layer, tab[base + DNF_ROW + k], rows, :],
                lambda k: W[layer, 1, tab[base + DNF_PERM + k]],
            )

            def mixed(b):
                v = ACT[op, b, rows, :].astype(f32)
                return (v + PS[tab[base + DN_LAST + b]]).astype(bf16)

            @pl.when(jnp.logical_not(final))
            def _():
                def put(b, c):
                    OUT[op, b, rows, :] = mixed(b)
                    return c

                lax.fori_loop(0, DB, put, 0, unroll=True)

            @pl.when(jnp.logical_and(final, op == 0))
            def _():
                def put(b, c):
                    ACT[1, b, rows, :] = mixed(b)
                    return c

                lax.fori_loop(0, DB, put, 0, unroll=True)

            @pl.when(jnp.logical_and(final, op == 1))
            def _():
                def put(b, c):
                    residue = mixed(b).astype(f32) - TG[b, rows, :].astype(f32)
                    ACT[2, b, rows, :] = residue.astype(bf16)
                    return c

                lax.fori_loop(0, DB, put, 0, unroll=True)

        @pl.when(op >= 2)
        def _():
            inputs = 3 - op
            for b in range(DB):
                COT[layer, b, rows, :] = ACT[op, b, rows, :]
            def slope_times(j):
                g = PS[tab[base + VB_LAST + j]]
                result = (g * S[layer, j, rows, :].astype(f32)).astype(bf16)

                def store():
                    S[layer, j, rows, :] = result

                return store

            chain(
                keep_base + K_VB,
                lambda k: COT[layer, tab[base + VB_COL + k], rows, :],
                lambda k: WT[layer, 1, k],
                then=slope_times,
            )

            @pl.when(jnp.logical_not(jnp.logical_and(final, op == 3)))
            def _():
                chain(
                    keep_base + K_UB,
                    lambda k: S[layer, tab[base + UB_COL + k], rows, :],
                    lambda k: WT[layer, 0, k],
                )
                factor = factor_of(inputs)

                def couple(b, acc):
                    v = ACT[inputs, b, rows, :].astype(f32)
                    return acc + v * PS[tab[base + UB_LAST + b]]

                coupling = lax.fori_loop(0, DB, couple, jnp.zeros((R, BS), f32), unroll=True)
                coupling = jnp.sum(coupling, axis=-1, keepdims=True) * (1.0 / D)
                pull = factor * factor * factor * coupling

                def downstream(b):
                    v = ACT[inputs, b, rows, :].astype(f32)
                    g = PS[tab[base + UB_LAST + b]]
                    return (ACT[op, b, rows, :].astype(f32) + factor * g - v * pull).astype(bf16)

                @pl.when(jnp.logical_not(final))
                def _():
                    def put(b, c):
                        OUT[op, b, rows, :] = downstream(b)
                        return c

                    lax.fori_loop(0, DB, put, 0, unroll=True)

                @pl.when(final)
                def _():
                    def put(b, c):
                        ACT[3, b, rows, :] = downstream(b)
                        return c

                    lax.fori_loop(0, DB, put, 0, unroll=True)

        @pl.when(jnp.logical_not(final))
        def _():
            link(op, chunk, target).start()

    def pair(lhs, rhs):
        return lax.dot_general(lhs, rhs, (((0,), (0,)), ((), ())), preferred_element_type=f32)

    def weight_gradient(role, proj):
        base = jnp.where(role == 0, own, 1 - own) * TABLE

        def blocks(outer, c):
            parts = []
            for u in range(16):
                k = outer * 16 + u
                if proj == 0:
                    lhs = NORM[role, tab[base + U_ROW + k]]
                    rhs = S[role, tab[base + UB_COL + k]]
                else:
                    lhs = H[role, tab[base + V_ROW + k]]
                    rhs = COT[role, tab[base + VB_COL + k]]
                parts.append(pair(lhs, rhs))
            for v in range(8):
                for d in range(16):
                    both = jnp.concatenate(
                        [p[8 * d : 8 * d + 8] for p in parts[2 * v : 2 * v + 2]], axis=0
                    )
                    of_core, of_y, of_z = d % 2, d // 4, (d // 2) % 2
                    place = of_core * 8 + (of_y * 2 + of_z if proj == 0 else of_z * 4 + of_y)
                    W[role, proj, place * SLICE + outer, 16 * v : 16 * v + 16, :] = both.astype(bf16)
            return c

        lax.fori_loop(0, SLICE, blocks, 0)

    mine = core * 8 * SLICE

    def unit(proj, of_y, of_z):
        return mine + (of_y * 2 + of_z if proj == 0 else of_z * 4 + of_y) * SLICE

    CORE, FAR_UP, FAR_DOWN, UP, DOWN, Z, MIRROR, CORE_STAY = range(8)
    half = SLICE // 2
    copies = (
        (
            ((1 - core) * 8 * SLICE, 0, 48, peer_core),
            (unit(0, y_far, 0), 48, SLICE, peer_up),
            (unit(0, y_far, 1), 54, SLICE, peer_down),
            (unit(0, y_up, 0), 60, 2 * SLICE, peer_up),
            (unit(0, y_down, 0), 72, 2 * SLICE, peer_down),
            (unit(0, y, 1 - z_lo), 84, SLICE, peer_z),
            (unit(0, y, z_lo), 90, SLICE, mirror),
        ),
        (
            ((1 - core) * 8 * SLICE + (1 - z_lo) * 4 * SLICE, 0, 24, peer_core),
            (unit(1, y_far, z_lo), 48, half, peer_up),
            (unit(1, y_far, z_lo) + half, 51, half, peer_down),
            (unit(1, y_up, z_lo), 54, SLICE, peer_up),
            (unit(1, y_down, z_lo), 60, SLICE, peer_down),
            (unit(1, 0, 1 - z_lo), 66, 4 * SLICE, peer_z),
            (unit(1, y, z_lo), 90, SLICE, mirror),
            ((1 - core) * 8 * SLICE + z_lo * 4 * SLICE, 24, 24, peer_core),
        ),
    )

    def share_copy(role, proj, number):
        source, landing, count, peer = copies[proj][number]
        return pltpu.make_async_remote_copy(
            src_ref=W.at[role, proj, pl.ds(source, count)],
            dst_ref=WT.at[role, proj, pl.ds(landing, count)],
            send_sem=share_send.at[role, proj, number],
            recv_sem=share_recv.at[role, proj, number],
            device_id=peer,
            device_id_type=MESH,
        )

    def add(role, proj, place, *numbers):
        for number in numbers:
            share_copy(role, proj, number).wait_recv()

        def step(n, c):
            total = W[role, proj, place + n].astype(f32)
            for number in numbers:
                total = total + WT[role, proj, copies[proj][number][1] + n].astype(f32)
            W[role, proj, place + n] = total.astype(bf16)
            return c

        lax.fori_loop(0, copies[proj][numbers[0]][2], step, 0, unroll=3)

    def send(role, proj, *numbers):
        for number in numbers:
            share_copy(role, proj, number).start()

    def action(code):
        step, role = (code - 4 * chunks) // 2, (code - 4 * chunks) % 2
        owner = own == role

        def wait_ready(number):
            pl.semaphore_wait(ready_sem.at[role, number], 1)

        def send_mirror(proj):
            @pl.when(jnp.logical_not(owner))
            def _():
                if proj == 0:
                    wait_ready(4)
                send(role, proj, MIRROR)

        @pl.when(step == 0)
        def _():
            for number, peer in enumerate(peers[:4]):
                pl.semaphore_signal(ready_sem.at[role, number], inc=1, device_id=peer, device_id_type=MESH)

            @pl.when(owner)
            def _():
                pl.semaphore_signal(ready_sem.at[role, 4], inc=1, device_id=mirror, device_id_type=MESH)

            weight_gradient(role, 1)
            wait_ready(0)
            send(role, 1, CORE)
            weight_gradient(role, 0)
            send(role, 0, CORE)
            send(role, 1, CORE_STAY)

        @pl.when(step == 1)
        def _():
            add(role, 1, unit(1, 0, 1 - z_lo), CORE)
            wait_ready(3)
            send(role, 1, Z)
            add(role, 0, mine, CORE)
            wait_ready(1)
            wait_ready(2)
            send(role, 0, FAR_UP, FAR_DOWN)
            add(role, 1, unit(1, 0, z_lo), CORE_STAY)

        @pl.when(step == 2)
        def _():
            add(role, 0, unit(0, y_up, 0), FAR_UP)
            send(role, 0, UP)
            add(role, 0, unit(0, y_down, 1), FAR_DOWN)
            send(role, 0, DOWN)

        @pl.when(step == 3)
        def _():
            add(role, 0, unit(0, y, 0), UP, DOWN)
            send(role, 0, Z)
            add(role, 1, unit(1, 0, z_lo), Z)
            send(role, 1, FAR_UP, FAR_DOWN)

        @pl.when(step == 4)
        def _():
            add(role, 1, unit(1, y_up, z_lo), FAR_UP)
            send(role, 1, UP)
            add(role, 1, unit(1, y_down, z_lo) + half, FAR_DOWN)
            send(role, 1, DOWN)
            add(role, 0, unit(0, y, z_lo), Z)
            send_mirror(0)

        @pl.when(step == 5)
        def _():
            add(role, 1, unit(1, y, z_lo), UP, DOWN)
            send_mirror(1)

        @pl.when(jnp.logical_and(step == 6, owner))
        def _():
            for proj in range(2):
                share_copy(role, proj, MIRROR).wait_recv()
                for n in range(SLICE):
                    there = WT[role, proj, 90 + n].astype(f32)
                    sums_out[proj, n] = W[role, proj, unit(proj, y, z_lo) + n].astype(f32) + there

    def turn(i, carry):
        code = jnp.int32(0)
        for t in range(len(sequences[0])):
            code = jnp.where(i == t, pick(stage, [o[t] for o in sequences]), code)

        @pl.when(i == jnp.where(stage < 2, chunks, 0))
        def _():
            transpose_weights()

        @pl.when(code < 4 * chunks)
        def _():
            item(code)

        @pl.when(code >= 4 * chunks)
        def _():
            action(code)

        return carry

    lax.fori_loop(0, len(sequences[0]), turn, 0)

    def drain(i, carry):
        op, chunk = i // chunks, i % chunks
        even = op % 2 == 0
        target = jnp.where(even, upper, lower)
        final = jnp.where(even, stage == STAGES - 1, stage == 0)

        @pl.when(jnp.logical_not(final))
        def _():
            link(op, chunk, target).wait_send()

        return carry

    lax.fori_loop(0, 4 * chunks, drain, 0)
    for role in range(2):
        for proj in range(2):
            for number in range(MIRROR):
                share_copy(role, proj, number).wait_send()
            if proj == 1:
                share_copy(role, proj, CORE_STAY).wait_send()

            @pl.when(own != role)
            def _(role=role, proj=proj):
                share_copy(role, proj, MIRROR).wait_send()


def adam_update(grad_sum, master, moment, variance, token_total):
    gradient = grad_sum / token_total
    moment_next = beta_first * moment + (1.0 - beta_first) * gradient
    variance_next = beta_second * variance + (1.0 - beta_second) * gradient * gradient
    corrected = moment_next / (1.0 - beta_first**update_count)
    spread = jnp.sqrt(variance_next / (1.0 - beta_second**update_count))
    step_direction = corrected / (spread + adam_eps)
    return (step_direction, master - learn_rate * (step_direction + decay_rate * master))


def shards(tokens, targets, weights, pattern, master, moment, variance):
    dp_size = lax.axis_size("dp")
    row_count = tokens.shape[1] * tokens.shape[2]
    chunks = row_count // ROWS

    index, keeps = tables(pattern[0])
    orders = make_orders(chunks, 2.6, 2.5, 4.5)
    smem = pl.BlockSpec(memory_space=pltpu.SMEM)
    anywhere = pl.BlockSpec(memory_space=pl.ANY)
    grads = pl.pallas_call(
        functools.partial(pipeline_kernel, chunks, make_sequences(chunks, orders)),
        out_shape=jax.ShapeDtypeStruct((2, SLICE, BS, BS), f32),
        in_specs=[smem, smem, anywhere, anywhere, anywhere],
        out_specs=pl.BlockSpec(memory_space=pltpu.VMEM),
        scratch_shapes=[
            pltpu.VMEM((2, 2, NNZ, BS, BS), bf16),
            pltpu.VMEM((2, 2, NNZ, BS, BS), bf16),
            pltpu.VMEM((4, DB, row_count, BS), bf16),
            pltpu.VMEM((4, DB, row_count, BS), bf16),
            pltpu.VMEM((2, DB, row_count, BS), bf16),
            pltpu.VMEM((2, DB, row_count, BS), bf16),
            pltpu.VMEM((2, FB, row_count, BS), bf16),
            pltpu.VMEM((2, FB, row_count, BS), bf16),
            pltpu.VMEM((DB, row_count, BS), bf16),
            pltpu.VMEM((NNZ + 1, ROWS, BS), f32),
            pltpu.SemaphoreType.DMA((2, 2)),
            pltpu.SemaphoreType.DMA((2, DB)),
            pltpu.SemaphoreType.DMA((4, chunks)),
            pltpu.SemaphoreType.DMA((4, chunks)),
            pltpu.SemaphoreType.DMA((2, 2, 8)),
            pltpu.SemaphoreType.DMA((2, 2, 8)),
            pltpu.SemaphoreType.REGULAR((2, 5)),
        ],
        compiler_params=pltpu.CompilerParams(
            collective_id=0, has_side_effects=True, vmem_limit_bytes=60 * 1024 * 1024
        ),
    )(index, keeps, tokens.reshape(2, row_count, D), targets.reshape(2, row_count, D), weights[0])

    token_total = 2 * row_count * dp_size
    step_direction, master_next = adam_update(
        grads.reshape(master.shape[1:]), master[0], moment[0], variance[0], token_total
    )
    return (step_direction[None], master_next[None])


def solution(mesh):
    return jax.shard_map(
        shards,
        mesh=mesh,
        in_specs=(
            P(None, None, "dp", None),
            P(None, None, "dp", None),
            P("section", None, None, None, None, None),
            P("section", None, None, None, None),
            P("section", None, None, "dp", None),
            P("section", None, None, "dp", None),
            P("section", None, None, "dp", None),
        ),
        out_specs=(P("section", None, None, "dp", None), P("section", None, None, "dp", None)),
        check_vma=False,
    )
```
